256 devices in a mesh: dp: 32 (over z_lo, y, core), mp: 8 (over x, z_hi).
Axes of the slice: x: 4, y: 4, z: 8 (z_hi: 2, z_lo: 4; z = z_hi * 4 + z_lo), core: 2. Of those that a mesh axis runs over, the one named last changes fastest.
Arguments:
- gradient: bfloat16 [32, 2, 96, 28672], P('dp', None, None, 'mp'), may hold values from -180 to 180
- feedback: float32 [32, 2, 96, 28672], P('dp', None, None, 'mp'), may hold values from -6 to 6
- right_initial: float32 [2, 28672, 32], P(None, 'mp'), may hold values from -6 to 6
Outputs:
- decoded: float32 [2, 96, 28672], P(None, None, 'mp')
- carried: float32 [32, 2, 96, 28672], P('dp', None, None, 'mp')
The draws below stay inside these ranges and needn't reach their ends.
All inputs are finite; a program needn't handle non-finite values.
Results may differ from the reference program's by a relative error of at most 0.0003.
Values sent between devices are 32-bit elements; how exact they have to be, the bound alone decides.
A program may use at most 64 MiB of HBM per device.

```python
import math
import jax
import jax.numpy as jnp
from jax import lax

FF = 28672
RANK = 32
MATS = 2
ROWS = 96
REPLICAS = 32


def draw_gradient(key, part):
    key = jax.random.fold_in(key, 1)
    key_rows, key_cols, key_main = jax.random.split(key, 3)
    spread = math.log(10.0)
    row_scale = jnp.exp(jax.random.uniform(key_rows, (1, MATS, ROWS, 1), jnp.float32, 0.0, spread)) / math.sqrt(10.0)
    row_trend = (3.0 ** (jnp.arange(ROWS, dtype=jnp.float32) / ROWS - 0.5)).reshape(1, 1, ROWS, 1)
    col_scale = jnp.exp(jax.random.uniform(key_cols, (1, MATS, 1, FF), jnp.float32, 0.0, spread)) / math.sqrt(10.0)
    entries = jnp.clip(jax.random.normal(key_main, (REPLICAS, MATS, ROWS, FF), jnp.float32), -4.0, 4.0)
    return (row_scale * row_trend * col_scale * entries).astype(jnp.bfloat16)


def levels(key, extent, pieces, least, largest):
    loudness, own = 1.0, jax.random.fold_in(key, 6)
    for dim, blocks in pieces:
        draws = jnp.exp(jax.random.uniform(jax.random.fold_in(own, dim), (blocks,), jnp.float32, least / len(pieces), largest / len(pieces)))
        loudness = loudness * jnp.repeat(draws, extent[dim] // blocks).reshape([-1 if axis == dim else 1 for axis in range(len(extent))])
    return loudness


def noise(stream_key, shape, scale, reach, cuts=(), kind=jnp.bfloat16):
    values = scale * jax.random.normal(stream_key, shape, jnp.float32)
    if cuts:
        values = values * levels(stream_key, shape, cuts, -0.22, 0.18)
    return jnp.clip(values, -reach, reach).astype(kind)


def setup_inputs(seed: int = 0) -> dict:
    splits = jax.random.split(jax.random.key(seed), 4)
    gradient = draw_gradient(jax.random.fold_in(splits[3], 71), 0)
    feedback = noise(splits[1], (REPLICAS, MATS, ROWS, FF), 1.0, 6.0, ((0, 32), (3, 8)), jnp.float32)
    right_initial = noise(splits[2], (MATS, FF, RANK), 1.0, 6.0, ((1, 8),), jnp.float32)
    return {"gradient": gradient, "feedback": feedback, "right_initial": right_initial}


def reference(gradient, feedback, right_initial):
    highest_precision_mode = lax.Precision.HIGHEST

    def p_term(loop_carry_state, pair):
        merged_gradient = pair[0].astype(jnp.float32) + pair[1]
        return (loop_carry_state + jnp.einsum('lqg,lgh->lqh', merged_gradient, right_initial, precision=highest_precision_mode), None)
    p_sum, _ = lax.scan(p_term, jnp.zeros((MATS, ROWS, RANK), jnp.float32), (gradient, feedback))
    p_full = p_sum / REPLICAS
    gram_matrix = jnp.einsum('mrk,mrl->mkl', p_full, p_full, precision=highest_precision_mode)
    factor_low = jnp.linalg.cholesky(gram_matrix)
    left_orthonormal = lax.linalg.triangular_solve(factor_low, p_full, left_side=False, lower=True, transpose_a=True)

    def q_term(loop_carry_state, pair):
        merged_gradient = pair[0].astype(jnp.float32) + pair[1]
        return (loop_carry_state + jnp.einsum('djs,djp->dsp', merged_gradient, left_orthonormal, precision=highest_precision_mode), None)
    q_sum, _ = lax.scan(q_term, jnp.zeros((MATS, FF, RANK), jnp.float32), (gradient, feedback))
    right_averaged = q_sum / REPLICAS
    decoded = jnp.einsum('gws,gos->gwo', left_orthonormal, right_averaged, precision=highest_precision_mode)

    def new_residual(pair):
        return pair[0].astype(jnp.float32) + pair[1] - decoded
    carried = lax.map(new_residual, (gradient, feedback))
    return (decoded, carried)
```

```python
import functools

import jax
import jax.numpy as jnp
from jax import lax
from jax.experimental import pallas as pl
from jax.experimental.pallas import tpu as pltpu
from jax.sharding import PartitionSpec as P

MESH = pl.DeviceIdType.MESH
F32 = jnp.float32
BF16 = jnp.bfloat16
MATS, ROWS, RANK, COLS = 2, 96, 32, 3584
WIDTH = 896
HALF = ROWS // 2
REPLICAS = 32
VMEM_BYTES = 48 << 20


def split(a):
    hi = a.astype(BF16)
    return hi, (a - hi.astype(F32)).astype(BF16)


def dot(a, b, contract):
    return lax.dot_general(a, b, ((contract[0], contract[1]), ((), ())), preferred_element_type=F32)


def exact(a, b, contract):
    return lax.dot_general(
        a, b, ((contract[0], contract[1]), ((), ())), precision=lax.Precision.HIGHEST, preferred_element_type=F32
    )


def left_times_inverse(p_t):
    gram = exact(p_t, p_t, ((1,), (1,)))
    row = lax.broadcasted_iota(jnp.int32, (RANK, RANK), 0)
    col = lax.broadcasted_iota(jnp.int32, (RANK, RANK), 1)
    eye = jnp.where(row == col, 1.0, 0.0).astype(F32)
    inv = eye
    for k in range(RANK - 1):
        scale = 1.0 / gram[k : k + 1, k : k + 1]
        g_row = gram[k : k + 1, :] * scale
        i_row = inv[k : k + 1, :] * scale
        factor = jnp.where(row[:, 0:1] > k, gram[:, k : k + 1], 0.0)
        gram = gram - factor * g_row
        inv = inv - factor * i_row
    diag = jnp.sum(gram * eye, axis=1, keepdims=True)
    l_inv = inv * lax.rsqrt(diag)
    orth_t = exact(l_inv, p_t, ((1,), (0,)))
    return exact(l_inv, orth_t, ((0,), (0,)))


def reduce_kernel(
    g_hbm, f_hbm, r_hbm, comb, q_all, w_out,
    g_buf, f_buf, r_buf, c_recv, s_buf, r1, r2, p_own, p_core, p_y, p_x, p_z, p_full, q_part, z_part,
    load_sem, cs_sem, cr_sem, ss_sem, sr_sem, ps_sem, pr_sem, zs_sem, zr_sem, as_sem, ar_sem,
):
    d = lax.axis_index("dp")
    m = lax.axis_index("mp")
    zl, y, c = d // 8, (d // 2) % 4, d % 2
    x, zh = m // 2, m % 2
    z = zh * 4 + zl

    def at(zl_=zl, y_=y, c_=c, x_=x, zh_=zh):
        return (zl_ * 8 + y_ * 2 + c_, x_ * 2 + zh_)

    def z_peer(k):
        to = (z + k) % 8
        return at(zl_=to % 4, zh_=to // 4)

    core_peer = at(c_=1 - c)
    y_next, y_prev = (y + 1) % 4, (y + 3) % 4
    y_far = (y + 2) % 4
    y_peers = [at(y_=(y + k) % 4) for k in (1, 2, 3)]
    x_peers = [at(x_=(x + k) % 4) for k in (1, 2, 3)]
    z_peers = [z_peer(k) for k in range(1, 8)]

    sends = []

    def remote(src, dst, ssem, rsem, to):
        return pltpu.make_async_remote_copy(
            src_ref=src, dst_ref=dst, send_sem=ssem, recv_sem=rsem, device_id=to, device_id_type=MESH
        )

    def send(src, dst, ssem, rsem, to):
        copy = remote(src, dst, ssem, rsem, to)
        copy.start()
        sends.append(copy)

    def landed(dst, ssem, rsem):
        remote(dst, dst, ssem, rsem, core_peer).wait_recv()

    barrier = pltpu.get_barrier_semaphore()
    peers = [core_peer] + y_peers + x_peers + z_peers
    for to in peers:
        pl.semaphore_signal(barrier, inc=1, device_id=to, device_id_type=MESH)

    def chunk_cols(cc, yy):
        return pl.ds(pl.multiple_of((2 * cc + yy % 2) * WIDTH, 128), WIDTH)

    loads = []
    order = [(which, yy) for which in (0, 1) for yy in range(4)]
    for i, (which, yy) in enumerate(order):
        cc = 1 - c if which == 0 else c
        cols = chunk_cols(cc, yy)
        mat = yy // 2
        copies = [
            pltpu.make_async_copy(f_hbm.at[0, mat, :, cols], f_buf.at[i], load_sem.at[0, i]),
            pltpu.make_async_copy(g_hbm.at[0, mat, :, cols], g_buf.at[i], load_sem.at[1, i]),
            pltpu.make_async_copy(r_hbm.at[mat, :, cols], r_buf.at[i], load_sem.at[2, i]),
        ]
        for copy in copies:
            copy.start()
        loads.append(copies)

    p_sum = [jnp.zeros((2 * RANK, ROWS), F32) for _ in range(MATS)]
    for i, (which, yy) in enumerate(order):
        cc = 1 - c if which == 0 else c
        for copy in loads[i]:
            copy.wait()
        both = g_buf[i].astype(F32) + f_buf[i]
        comb[cc, yy] = both
        if i == 0:
            pl.semaphore_wait(barrier, len(peers))
        if which == 0:
            send(comb.at[cc, yy], c_recv.at[yy], cs_sem.at[yy], cr_sem.at[yy], core_peer)
        hi, lo = split(both)
        right = jnp.concatenate(split(r_buf[i]), axis=0)
        mat = yy // 2
        p_sum[mat] += dot(right, hi, ((1,), (1,))) + dot(right, lo, ((1,), (1,)))

    p_own[...] = jnp.zeros(p_own.shape, F32)
    for mat in range(MATS):
        p_own[mat, :, 0:ROWS] = p_sum[mat][:RANK] + p_sum[mat][RANK:]
    send(p_own.at[1 - c], p_core, ps_sem.at[0], pr_sem.at[0], core_peer)
    landed(p_core, ps_sem.at[0], pr_sem.at[0])
    p_y[y] = p_own[c] + p_core[...]
    for k, to in enumerate(y_peers):
        send(p_y.at[y], p_y.at[y], ps_sem.at[1 + k], pr_sem.at[1 + y], to)

    for yy in range(4):
        landed(c_recv.at[yy], cs_sem.at[yy], cr_sem.at[yy])
        s_buf[yy] = comb[c, yy] + c_recv[yy]
    top, low = pl.ds(0, HALF), pl.ds(HALF, HALF)
    to_next, to_prev = at(y_=y_next), at(y_=y_prev)
    send(s_buf.at[y_far, top], r1.at[0], ss_sem.at[0], sr_sem.at[0], to_next)
    send(s_buf.at[y_far, low], r1.at[1], ss_sem.at[1], sr_sem.at[1], to_prev)
    send(s_buf.at[y_next, low], r2.at[0], ss_sem.at[2], sr_sem.at[2], to_next)
    send(s_buf.at[y_prev, top], r2.at[1], ss_sem.at[3], sr_sem.at[3], to_prev)

    for k in (1, 2, 3):
        src = (y + k) % 4
        landed(p_y.at[src], ps_sem.at[0], pr_sem.at[1 + src])
    p_x[x] = (p_y[0] + p_y[1]) + (p_y[2] + p_y[3])
    for k, to in enumerate(x_peers):
        send(p_x.at[x], p_x.at[x], ps_sem.at[4 + k], pr_sem.at[5 + x], to)

    landed(r1.at[0], ss_sem.at[0], sr_sem.at[0])
    s_buf[y_next, top] += r1[0]
    send(s_buf.at[y_next, top], r2.at[2], ss_sem.at[4], sr_sem.at[4], to_next)
    landed(r1.at[1], ss_sem.at[1], sr_sem.at[1])
    s_buf[y_prev, low] += r1[1]
    send(s_buf.at[y_prev, low], r2.at[3], ss_sem.at[5], sr_sem.at[5], to_prev)

    for k in (1, 2, 3):
        src = (x + k) % 4
        landed(p_x.at[src], ps_sem.at[0], pr_sem.at[5 + src])
    p_z[z] = (p_x[0] + p_x[1]) + (p_x[2] + p_x[3])
    for k, to in enumerate(z_peers):
        send(p_z.at[z], p_z.at[z], ps_sem.at[7 + k], pr_sem.at[9 + z], to)
    for k in range(1, 8):
        src = (z + k) % 8
        landed(p_z.at[src], ps_sem.at[0], pr_sem.at[9 + src])
    total = ((p_z[0] + p_z[1]) + (p_z[2] + p_z[3])) + ((p_z[4] + p_z[5]) + (p_z[6] + p_z[7]))
    p_full[c] = total * (1.0 / REPLICAS)
    send(p_full.at[c], p_full.at[c], ps_sem.at[14], pr_sem.at[17], core_peer)

    for i in range(2):
        landed(r2.at[i], ss_sem.at[0], sr_sem.at[2 + i])
        landed(r2.at[2 + i], ss_sem.at[0], sr_sem.at[4 + i])
    chunk_top = (s_buf[y, top] + r2[1]) + r2[2]
    chunk_low = (s_buf[y, low] + r2[0]) + r2[3]
    landed(p_full.at[1 - c], ps_sem.at[0], pr_sem.at[17])

    left = jnp.concatenate(split(p_full[y // 2][:, :ROWS]), axis=0)
    hi, lo = split(jnp.concatenate([chunk_top, chunk_low], axis=0))
    prod = dot(left, hi, ((1,), (0,))) + dot(left, lo, ((1,), (0,)))
    q_part[...] = (prod[:RANK] + prod[RANK:]).reshape(4, 8, WIDTH)
    for k in (1, 2, 3):
        to = (zl + k) % 4
        send(q_part.at[to], z_part.at[zl], zs_sem.at[k], zr_sem.at[zl], at(zl_=to))
    z_part[zl] = q_part[zl]

    for mat in range(MATS):
        w_out[mat] = left_times_inverse(p_full[mat][:, :ROWS]) * (1.0 / REPLICAS)

    for k in (1, 2, 3):
        src = (zl + k) % 4
        landed(z_part.at[src], zs_sem.at[0], zr_sem.at[src])
    q_all[c, y, zl] = (z_part[0] + z_part[1]) + (z_part[2] + z_part[3])

    for k in (1, 2, 3):
        to = (zl + k) % 4
        send(q_all.at[c, y, zl], q_all.at[c, y, zl], as_sem.at[k], ar_sem.at[zl], at(zl_=to))
    for k in (1, 2, 3):
        src = (zl + k) % 4
        landed(q_all.at[c, y, src], as_sem.at[0], ar_sem.at[src])
    send(q_all.at[c, y], q_all.at[c, y], as_sem.at[4], ar_sem.at[4], to_next)
    send(q_all.at[c, y], q_all.at[c, y], as_sem.at[5], ar_sem.at[5], to_prev)
    send(q_all.at[c, y], q_all.at[c, y], as_sem.at[6], ar_sem.at[8], core_peer)
    first, second = pl.ds(0, 2), pl.ds(2, 2)
    landed(q_all.at[c, y_prev], as_sem.at[0], ar_sem.at[4])
    send(q_all.at[c, y_prev, first], q_all.at[c, y_prev, first], as_sem.at[7], ar_sem.at[6], to_next)
    send(q_all.at[c, y_prev], q_all.at[c, y_prev], as_sem.at[8], ar_sem.at[9], core_peer)
    landed(q_all.at[c, y_next], as_sem.at[0], ar_sem.at[5])
    send(q_all.at[c, y_next, second], q_all.at[c, y_next, second], as_sem.at[9], ar_sem.at[7], to_prev)
    send(q_all.at[c, y_next], q_all.at[c, y_next], as_sem.at[10], ar_sem.at[10], core_peer)
    landed(q_all.at[c, y_far, first], as_sem.at[0], ar_sem.at[6])
    landed(q_all.at[c, y_far, second], as_sem.at[0], ar_sem.at[7])
    send(q_all.at[c, y_far], q_all.at[c, y_far], as_sem.at[11], ar_sem.at[11], core_peer)
    for i, yy in enumerate((y, y_prev, y_next, y_far)):
        landed(q_all.at[1 - c, yy], as_sem.at[0], ar_sem.at[8 + i])
    for copy in sends:
        copy.wait_send()


def decode_kernel(comb, q_all, w_ref, decoded, carried, d_buf, c_buf, sem):
    left = []
    for mat in range(MATS):
        hi, lo = split(w_ref[mat].T)
        left.append(jnp.concatenate([hi, lo, hi, lo], axis=1))
    copies = []
    for i in range(8):
        cc, yy = i // 4, i % 4
        mat, cols = yy // 2, pl.ds((2 * cc + yy % 2) * WIDTH, WIDTH)
        hi, lo = split(q_all[cc, yy].reshape(RANK, WIDTH))
        out = dot(left[mat], jnp.concatenate([hi, hi, lo, lo], axis=0), ((1,), (0,)))
        d_buf[i] = out
        copies.append(pltpu.make_async_copy(d_buf.at[i], decoded.at[mat, :, cols], sem.at[0, i]))
        copies[-1].start()
        c_buf[i] = comb[cc, yy] - out
        copies.append(pltpu.make_async_copy(c_buf.at[i], carried.at[0, mat, :, cols], sem.at[1, i]))
        copies[-1].start()
    for copy in copies:
        copy.wait()


def per_device(gradient, feedback, right_initial):
    right_t = jnp.swapaxes(right_initial, 1, 2)
    vmem = pl.BlockSpec(memory_space=pltpu.VMEM)
    hbm = pl.BlockSpec(memory_space=pltpu.HBM)
    dma = pltpu.SemaphoreType.DMA
    comb, q_all, w = pl.pallas_call(
        reduce_kernel,
        name="reduce",
        out_shape=(
            jax.ShapeDtypeStruct((2, 4, ROWS, WIDTH), F32),
            jax.ShapeDtypeStruct((2, 4, 4, 8, WIDTH), F32),
            jax.ShapeDtypeStruct((MATS, RANK, ROWS), F32),
        ),
        in_specs=[hbm] * 3,
        out_specs=(vmem, vmem, vmem),
        scratch_shapes=[
            pltpu.VMEM((8, ROWS, WIDTH), BF16),
            pltpu.VMEM((8, ROWS, WIDTH), F32),
            pltpu.VMEM((8, RANK, WIDTH), F32),
            pltpu.VMEM((4, ROWS, WIDTH), F32),
            pltpu.VMEM((4, ROWS, WIDTH), F32),
            pltpu.VMEM((2, HALF, WIDTH), F32),
            pltpu.VMEM((4, HALF, WIDTH), F32),
            pltpu.VMEM((MATS, RANK, 128), F32),
            pltpu.VMEM((RANK, 128), F32),
            pltpu.VMEM((4, RANK, 128), F32),
            pltpu.VMEM((4, RANK, 128), F32),
            pltpu.VMEM((8, RANK, 128), F32),
            pltpu.VMEM((MATS, RANK, 128), F32),
            pltpu.VMEM((4, 8, WIDTH), F32),
            pltpu.VMEM((4, 8, WIDTH), F32),
            dma((3, 8)),
            dma((4,)),
            dma((4,)),
            dma((6,)),
            dma((6,)),
            dma((15,)),
            dma((18,)),
            dma((4,)),
            dma((4,)),
            dma((12,)),
            dma((12,)),
        ],
        compiler_params=pltpu.CompilerParams(
            collective_id=0, has_side_effects=True, vmem_limit_bytes=VMEM_BYTES
        ),
    )(gradient, feedback, right_t)
    return pl.pallas_call(
        decode_kernel,
        name="decode",
        out_shape=(
            jax.ShapeDtypeStruct((MATS, ROWS, COLS), F32),
            jax.ShapeDtypeStruct((1, MATS, ROWS, COLS), F32),
        ),
        in_specs=[vmem] * 3,
        out_specs=(hbm, hbm),
        scratch_shapes=[
            pltpu.VMEM((8, ROWS, WIDTH), F32),
            pltpu.VMEM((8, ROWS, WIDTH), F32),
            dma((2, 8)),
        ],
        compiler_params=pltpu.CompilerParams(vmem_limit_bytes=VMEM_BYTES),
    )(comb, q_all, w)


def solution(mesh):
    placed = (P("dp", None, None, "mp"), P("dp", None, None, "mp"), P(None, "mp", None))
    return jax.shard_map(
        per_device,
        mesh=mesh,
        in_specs=placed,
        out_specs=(P(None, None, "mp"), P("dp", None, None, "mp")),
        check_vma=False,
    )
```

```python
import functools

import jax
import jax.numpy as jnp
from jax import lax
from jax.experimental import pallas as pl
from jax.experimental.pallas import tpu as pltpu
from jax.sharding import PartitionSpec as P

MESH = pl.DeviceIdType.MESH
F32 = jnp.float32
BF16 = jnp.bfloat16
MATS, ROWS, RANK, COLS = 2, 96, 32, 3584
WIDTH = 896
HALF = ROWS // 2
REPLICAS = 32
SENDS = 64
VMEM_BYTES = 32 << 20


def split(a):
    hi = a.astype(BF16)
    return hi, (a - hi.astype(F32)).astype(BF16)


def dot(a, b, contract):
    return lax.dot_general(a, b, ((contract[0], contract[1]), ((), ())), preferred_element_type=F32)


def exact(a, b, contract):
    return lax.dot_general(
        a, b, ((contract[0], contract[1]), ((), ())), precision=lax.Precision.HIGHEST, preferred_element_type=F32
    )


def left_times_inverses(p_ts):
    row = lax.broadcasted_iota(jnp.int32, (RANK, RANK), 0)
    col = lax.broadcasted_iota(jnp.int32, (RANK, RANK), 1)
    eye = jnp.where(row == col, 1.0, 0.0).astype(F32)
    grams = [exact(p_t, p_t, ((1,), (1,))) for p_t in p_ts]
    invs = [eye for _ in p_ts]
    for k in range(RANK - 1):
        below = row > k
        for i, (gram, inv) in enumerate(zip(grams, invs)):
            scale = 1.0 / gram[k : k + 1, k : k + 1]
            factor = jnp.where(below, jnp.broadcast_to(gram[:, k : k + 1], (RANK, RANK)), 0.0)
            grams[i] = gram - factor * (gram[k : k + 1, :] * scale)
            invs[i] = inv - factor * (inv[k : k + 1, :] * scale)
    out = []
    for gram, inv, p_t in zip(grams, invs, p_ts):
        diag = jnp.sum(gram * eye, axis=1, keepdims=True)
        l_inv = inv * lax.rsqrt(diag)
        orth_t = exact(l_inv, p_t, ((1,), (0,)))
        out.append(exact(l_inv, orth_t, ((0,), (0,))))
    return out


def decode(left, q):
    hi, lo = split(q)
    return dot(left, jnp.concatenate([hi, hi, lo, lo], axis=0), ((1,), (0,)))


class Net:
    def __init__(self, send_sem, recv_sem):
        self.send_sem, self.recv_sem = send_sem, recv_sem
        self.sent, self.due, self.last = [], {}, []

    def copy(self, src, dst, i, j, to):
        return pltpu.make_async_remote_copy(
            src_ref=src,
            dst_ref=dst,
            send_sem=self.send_sem.at[i],
            recv_sem=self.recv_sem.at[j],
            device_id=to,
            device_id_type=MESH,
        )

    def send(self, tag, src, dst, mine, to):
        i = len(self.sent)
        copy = self.copy(src, dst, i, i, to)
        copy.start()
        self.sent.append(copy)
        self.due.setdefault(tag, []).append((mine, i, to))

    def take(self, tag):
        for mine, i, to in self.due.pop(tag):
            self.copy(mine, mine, i, i, to).wait_recv()

    def at_end(self, step):
        self.last.append(step)

    def finish(self):
        for tag in list(self.due):
            self.take(tag)
        for copy in self.sent:
            copy.wait_send()
        for step in self.last:
            step()


def tree_sum(ref, n):
    terms = [ref[i] for i in range(n)]
    while len(terms) > 1:
        terms = [a + b for a, b in zip(terms[::2], terms[1::2])]
    return terms[0]


def reduce_kernel(
    g_hbm, f_hbm, r_hbm, comb, q_all, w_out, decoded, carried,
    g_buf, f_buf, r_buf, c_recv, s_buf, r1, r2, p_own, p_core, p_y, p_x, p_z, p_full, q_part, z_part,
    load_sem, send_sem, recv_sem,
):
    d = lax.axis_index("dp")
    m = lax.axis_index("mp")
    zl, y, c = d // 8, (d // 2) % 4, d % 2
    x, zh = m // 2, m % 2
    z = zh * 4 + zl
    net = Net(send_sem, recv_sem)
    send, take = net.send, net.take

    def at(zl_=zl, y_=y, c_=c, x_=x, zh_=zh):
        return (zl_ * 8 + y_ * 2 + c_, x_ * 2 + zh_)

    def y_at(k):
        return at(y_=(y + k) % 4)

    def x_at(k):
        return at(x_=(x + k) % 4)

    def z_at(k):
        to = (z + k) % 8
        return at(zl_=to % 4, zh_=to // 4)

    def zl_at(k):
        return at(zl_=(zl + k) % 4)

    core_peer = at(c_=1 - c)
    y_next, y_prev, y_far = (y + 1) % 4, (y + 3) % 4, (y + 2) % 4

    barrier = pltpu.get_barrier_semaphore()
    peers = [core_peer] + [f(k) for f, n in ((y_at, 4), (x_at, 4), (z_at, 8)) for k in range(1, n)]
    for to in peers:
        pl.semaphore_signal(barrier, inc=1, device_id=to, device_id_type=MESH)

    loads = []
    order = [(which, yy) for which in (0, 1) for yy in range(4)]
    for i, (which, yy) in enumerate(order):
        cc = 1 - c if which == 0 else c
        cols = pl.ds(pl.multiple_of((2 * cc + yy % 2) * WIDTH, 128), WIDTH)
        mat = yy // 2
        copies = [
            pltpu.make_async_copy(f_hbm.at[0, mat, :, cols], f_buf.at[i], load_sem.at[0, i]),
            pltpu.make_async_copy(g_hbm.at[0, mat, :, cols], g_buf.at[i], load_sem.at[1, i]),
            pltpu.make_async_copy(r_hbm.at[mat, :, cols], r_buf.at[i], load_sem.at[2, i]),
        ]
        for copy in copies:
            copy.start()
        loads.append(copies)
    p_sum = [jnp.zeros((2 * RANK, ROWS), F32) for _ in range(MATS)]
    for i, (which, yy) in enumerate(order):
        cc = 1 - c if which == 0 else c
        for copy in loads[i]:
            copy.wait()
        both = g_buf[i].astype(F32) + f_buf[i]
        comb[cc, yy] = both
        if i == 3:
            pl.semaphore_wait(barrier, len(peers))
            for part in range(4):
                send("core%d" % part, comb.at[cc, part], c_recv.at[part], c_recv.at[part], core_peer)
        hi, lo = split(both)
        right = jnp.concatenate(split(r_buf[i]), axis=0)
        mat = yy // 2
        p_sum[mat] += dot(right, hi, ((1,), (1,))) + dot(right, lo, ((1,), (1,)))

    p_own[...] = jnp.zeros(p_own.shape, F32)
    for mat in range(MATS):
        p_own[mat, :, 0:ROWS] = p_sum[mat][:RANK] + p_sum[mat][RANK:]
    send("p_core", p_own.at[1 - c], p_core, p_core, core_peer)
    take("p_core")
    p_y[y] = p_own[c] + p_core[...]
    for k in (1, 2, 3):
        send("p_y", p_y.at[y], p_y.at[y], p_y.at[(y + 4 - k) % 4], y_at(k))

    for yy in range(4):
        take("core%d" % yy)
        s_buf[yy] = comb[c, yy] + c_recv[yy]
    top, low = pl.ds(0, HALF), pl.ds(HALF, HALF)
    send("r_top", s_buf.at[y_far, top], r1.at[0], r1.at[0], y_at(1))
    send("r_low", s_buf.at[y_far, low], r1.at[1], r1.at[1], y_at(3))
    send("r_end", s_buf.at[y_next, low], r2.at[0], r2.at[0], y_at(1))
    send("r_end", s_buf.at[y_prev, top], r2.at[1], r2.at[1], y_at(3))

    take("p_y")
    p_x[x] = tree_sum(p_y, 4)
    for k in (1, 2, 3):
        send("p_x", p_x.at[x], p_x.at[x], p_x.at[(x + 4 - k) % 4], x_at(k))

    take("r_top")
    s_buf[y_next, top] += r1[0]
    send("r_end", s_buf.at[y_next, top], r2.at[2], r2.at[2], y_at(1))
    take("r_low")
    s_buf[y_prev, low] += r1[1]
    send("r_end", s_buf.at[y_prev, low], r2.at[3], r2.at[3], y_at(3))

    take("p_x")
    p_z[z] = tree_sum(p_x, 4)
    for k in range(1, 8):
        send("p_z", p_z.at[z], p_z.at[z], p_z.at[(z + 8 - k) % 8], z_at(k))
    take("p_z")
    p_full[c] = tree_sum(p_z, 8) * (1.0 / REPLICAS)
    send("p_full", p_full.at[c], p_full.at[c], p_full.at[1 - c], core_peer)
    take("p_full")
    take("r_end")
    chunk_top = (s_buf[y, top] + r2[1]) + r2[2]
    chunk_low = (s_buf[y, low] + r2[0]) + r2[3]

    left = jnp.concatenate(split(p_full[y // 2][:, :ROWS]), axis=0)
    hi, lo = split(jnp.concatenate([chunk_top, chunk_low], axis=0))
    prod = dot(left, hi, ((1,), (0,))) + dot(left, lo, ((1,), (0,)))
    q_part[...] = (prod[:RANK] + prod[RANK:]).reshape(2, 16, WIDTH)

    near = zl // 2
    far = 1 - near
    owner = (zl == 1) | (zl == 2)

    def to_owner(h):
        return net.copy(q_part.at[h], z_part.at[zl], SENDS + h, SENDS + zl, at(zl_=1 + h))

    def from_owner(k):
        mine = q_all.at[c, y, near]
        return net.copy(mine, mine, SENDS + 1 + k, SENDS + 4 + near, zl_at(k))

    def arrival(ref, i):
        return net.copy(ref, ref, SENDS, i, core_peer)

    for h in range(2):
        pl.when(zl != 1 + h)(to_owner(h).start)

    @net.at_end
    def _():
        for h in range(2):
            pl.when(zl != 1 + h)(to_owner(h).wait_send)

        @pl.when(owner)
        def _():
            for k in (1, 2, 3):
                from_owner(k).wait_send()

    for mat, left in enumerate(left_times_inverses([p_full[mat][:, :ROWS] for mat in range(MATS)])):
        hi, lo = split(left.T * (1.0 / REPLICAS))
        w_out[mat] = jnp.concatenate([hi, lo, hi, lo], axis=1)

    @pl.when(owner)
    def _():
        z_part[zl] = q_part[near]
        for k in (1, 2, 3):
            src = (zl + k) % 4
            arrival(z_part.at[src], SENDS + src).wait_recv()
        q_all[c, y, near] = tree_sum(z_part, 4)
        for k in (1, 2, 3):
            from_owner(k).start()

    @pl.when(jnp.logical_not(owner))
    def _():
        arrival(q_all.at[c, y, near], SENDS + 4 + near).wait_recv()

    def hand_on(tag, yy, half, yy_mine, core_mine, to):
        part = q_all.at[c, yy, half]
        send(tag, part, part, q_all.at[core_mine, yy_mine, half], to)

    for half, name in ((near, "near"), (far, "far")):
        if name == "far":
            arrival(q_all.at[c, y, far], SENDS + 4 + far).wait_recv()
        for k in (2, 1, 3):
            hand_on("%s%d" % (name, k), y, half, (y + 4 - k) % 4, c, y_at(k))
        hand_on(name + "core", y, half, y, 1 - c, core_peer)

    def decode_own(yy):
        out = decode(w_out[yy // 2], q_all[c, yy].reshape(RANK, WIDTH))
        decoded[yy] = out
        carried[yy] = comb[c, yy] - out

    for half, name in ((near, "near"), (far, "far")):
        for k in (1, 3, 2):
            take("%s%d" % (name, k))
            yy = (y + 4 - k) % 4
            hand_on(name + "core", yy, half, yy, 1 - c, core_peer)
        if name == "near":
            decode_own(y)
    for k in (1, 3, 2):
        decode_own((y + 4 - k) % 4)
    net.finish()


def write_kernel(comb, q_all, w_ref, own_decoded, own_carried, decoded, carried, d_buf, c_buf, sem):
    c = lax.axis_index("dp") % 2
    copies = []

    def write(i, cc, yy, d_ref, c_ref):
        cols = pl.ds(pl.multiple_of((2 * cc + yy % 2) * WIDTH, 128), WIDTH)
        for j, (ref, to) in enumerate(((d_ref, decoded.at[yy // 2, :, cols]), (c_ref, carried.at[0, yy // 2, :, cols]))):
            copies.append(pltpu.make_async_copy(ref, to, sem.at[j, i]))
            copies[-1].start()

    for yy in range(4):
        write(yy, c, yy, own_decoded.at[yy], own_carried.at[yy])
    for yy in range(4):
        out = decode(w_ref[yy // 2], q_all[1 - c, yy].reshape(RANK, WIDTH))
        d_buf[yy] = out
        c_buf[yy] = comb[1 - c, yy] - out
        write(4 + yy, 1 - c, yy, d_buf.at[yy], c_buf.at[yy])
    for copy in copies:
        copy.wait()


def reduce_call(gradient, feedback, right_initial, name="reduce", collective_id=0):
    right_t = jnp.swapaxes(right_initial, 1, 2)
    vmem = pl.BlockSpec(memory_space=pltpu.VMEM)
    hbm = pl.BlockSpec(memory_space=pltpu.HBM)
    dma = pltpu.SemaphoreType.DMA
    return pl.pallas_call(
        reduce_kernel,
        name=name,
        out_shape=(
            jax.ShapeDtypeStruct((2, 4, ROWS, WIDTH), F32),
            jax.ShapeDtypeStruct((2, 4, 2, 16, WIDTH), F32),
            jax.ShapeDtypeStruct((MATS, ROWS, 128), BF16),
            jax.ShapeDtypeStruct((4, ROWS, WIDTH), F32),
            jax.ShapeDtypeStruct((4, ROWS, WIDTH), F32),
        ),
        in_specs=[hbm] * 3,
        out_specs=(vmem,) * 5,
        scratch_shapes=[
            pltpu.VMEM((8, ROWS, WIDTH), BF16),
            pltpu.VMEM((8, ROWS, WIDTH), F32),
            pltpu.VMEM((8, RANK, WIDTH), F32),
            pltpu.VMEM((4, ROWS, WIDTH), F32),
            pltpu.VMEM((4, ROWS, WIDTH), F32),
            pltpu.VMEM((2, HALF, WIDTH), F32),
            pltpu.VMEM((4, HALF, WIDTH), F32),
            pltpu.VMEM((MATS, RANK, 128), F32),
            pltpu.VMEM((RANK, 128), F32),
            pltpu.VMEM((4, RANK, 128), F32),
            pltpu.VMEM((4, RANK, 128), F32),
            pltpu.VMEM((8, RANK, 128), F32),
            pltpu.VMEM((MATS, RANK, 128), F32),
            pltpu.VMEM((2, 16, WIDTH), F32),
            pltpu.VMEM((4, 16, WIDTH), F32),
            dma((3, 8)),
            dma((SENDS + 8,)),
            dma((SENDS + 8,)),
        ],
        compiler_params=pltpu.CompilerParams(
            collective_id=collective_id, has_side_effects=True, vmem_limit_bytes=VMEM_BYTES
        ),
    )(*(pltpu.with_memory_space_constraint(a, pltpu.HBM) for a in (gradient, feedback, right_t)))


def per_device(gradient, feedback, right_initial):
    vmem = pl.BlockSpec(memory_space=pltpu.VMEM)
    hbm = pl.BlockSpec(memory_space=pltpu.HBM)
    return pl.pallas_call(
        write_kernel,
        name="write",
        out_shape=(
            jax.ShapeDtypeStruct((MATS, ROWS, COLS), F32),
            jax.ShapeDtypeStruct((1, MATS, ROWS, COLS), F32),
        ),
        in_specs=[vmem] * 5,
        out_specs=(hbm, hbm),
        scratch_shapes=[
            pltpu.VMEM((4, ROWS, WIDTH), F32),
            pltpu.VMEM((4, ROWS, WIDTH), F32),
            pltpu.SemaphoreType.DMA((2, 8)),
        ],
        compiler_params=pltpu.CompilerParams(vmem_limit_bytes=VMEM_BYTES),
    )(*reduce_call(gradient, feedback, right_initial))


def solution(mesh):
    placed = (P("dp", None, None, "mp"), P("dp", None, None, "mp"), P(None, "mp", None))
    return jax.shard_map(
        per_device,
        mesh=mesh,
        in_specs=placed,
        out_specs=(P(None, None, "mp"), P("dp", None, None, "mp")),
        check_vma=False,
    )
```

```python
import jax
import jax.numpy as jnp
from jax import lax
from jax.experimental import pallas as pl
from jax.experimental.pallas import tpu as pltpu
from jax.sharding import PartitionSpec as P

MESH = pl.DeviceIdType.MESH
F32 = jnp.float32
BF16 = jnp.bfloat16
MATS, ROWS, RANK, COLS = 2, 96, 32, 3584
WIDTH = 896
PIECES = ((0, 512), (512, 384))
HALF = ROWS // 2
REPLICAS = 32
TAGS = 32
VMEM_BYTES = 32 << 20


def split(a):
    hi = a.astype(BF16)
    return hi, (a - hi.astype(F32)).astype(BF16)


def dot(a, b, contract):
    return lax.dot_general(a, b, ((contract[0], contract[1]), ((), ())), preferred_element_type=F32)


def exact(a, b, contract):
    return lax.dot_general(
        a, b, ((contract[0], contract[1]), ((), ())), precision=lax.Precision.HIGHEST, preferred_element_type=F32
    )


def left_times_inverse(p_t):
    gram = exact(p_t, p_t, ((1,), (1,)))
    row = lax.broadcasted_iota(jnp.int32, (RANK, RANK), 0)
    col = lax.broadcasted_iota(jnp.int32, (RANK, RANK), 1)
    eye = jnp.where(row == col, 1.0, 0.0).astype(F32)
    inv = eye
    for k in range(RANK - 1):
        scale = 1.0 / gram[k : k + 1, k : k + 1]
        factor = jnp.where(row > k, jnp.broadcast_to(gram[:, k : k + 1], (RANK, RANK)), 0.0)
        gram, inv = (a - factor * (a[k : k + 1, :] * scale) for a in (gram, inv))
    diag = jnp.sum(gram * eye, axis=1, keepdims=True)
    l_inv = inv * lax.rsqrt(diag)
    orth_t = exact(l_inv, p_t, ((1,), (0,)))
    return exact(l_inv, orth_t, ((0,), (0,)))


def decode(left, q):
    hi, lo = split(q)
    return dot(left, jnp.concatenate([hi, hi, lo, lo], axis=0), ((1,), (0,)))


class Net:
    def __init__(self, send_sem, recv_sem):
        self.send_sem, self.recv_sem = send_sem, recv_sem
        self.tags, self.due, self.sent, self.last = {}, {}, [], []

    def copy(self, tag, src, dst, to):
        return pltpu.make_async_remote_copy(
            src_ref=src,
            dst_ref=dst,
            send_sem=self.send_sem.at[0],
            recv_sem=self.recv_sem.at[self.tags.setdefault(tag, len(self.tags))],
            device_id=to,
            device_id_type=MESH,
        )

    def send(self, tag, src, dst, to):
        self.sent.append(self.copy(tag, src, dst, to))
        self.sent[-1].start()

    def landing(self, tag, ref, to):
        return self.copy(tag, ref, ref, to).wait_recv

    def expect(self, tag, ref, to):
        self.due[tag] = self.landing(tag, ref, to)

    def take(self, tag):
        self.due.pop(tag)()

    def at_end(self, step):
        self.last.append(step)

    def finish(self):
        for tag in list(self.due):
            self.take(tag)
        for copy in self.sent:
            copy.wait_send()
        for step in self.last:
            step()


def tree_sum(terms):
    while len(terms) > 1:
        terms = [a + b for a, b in zip(terms[::2], terms[1::2])]
    return terms[0]


def reduce_kernel(
    g_hbm, f_hbm, r_hbm, comb, q_all, w_out, decoded, carried,
    g_buf, f_buf, r_buf, c_recv, s_buf, r1, r2, p_own, p_core, p_mid, p_y, p_x, p_z, p_full, w_t, q_part, z_part,
    load_sem, send_sem, recv_sem,
):
    d = lax.axis_index("dp")
    m = lax.axis_index("mp")
    zl, y, c = d // 8, (d // 2) % 4, d % 2
    x, zh = m // 2, m % 2
    z = zh * 4 + zl
    net = Net(send_sem, recv_sem)
    send, take = net.send, net.take

    def at(zl_=zl, y_=y, c_=c, x_=x, zh_=zh):
        return (zl_ * 8 + y_ * 2 + c_, x_ * 2 + zh_)

    def y_at(k):
        return at(y_=(y + k) % 4)

    def x_at(k):
        return at(x_=(x + k) % 4)

    def z_at(k):
        to = (z + k) % 8
        return at(zl_=to % 4, zh_=to // 4)

    def zl_at(k):
        return at(zl_=(zl + k) % 4)

    core_peer = at(c_=1 - c)
    y_next, y_prev, y_far = (y + 1) % 4, (y + 3) % 4, (y + 2) % 4
    mat = y // 2

    pairs = [(1 - c, 1 - mat), (c, 1 - mat), (1 - c, mat), (c, mat)]
    loads = []
    for i, (cc, mm) in enumerate(pairs):
        cols = pl.ds(pl.multiple_of(cc * 2 * WIDTH, 128), 2 * WIDTH)
        loads.append(
            (
                pltpu.make_async_copy(f_hbm.at[0, mm, :, cols], f_buf.at[i], load_sem.at[i]),
                pltpu.make_async_copy(g_hbm.at[0, mm, :, cols], g_buf.at[i], load_sem.at[4 + i]),
            )
        )
    right_load = pltpu.make_async_copy(r_hbm, r_buf, load_sem.at[8])
    for copies in loads:
        for copy in copies:
            copy.start()
    right_load.start()

    barrier = pltpu.get_barrier_semaphore()
    peers = [core_peer] + [f(k) for f, n in ((y_at, 4), (x_at, 4), (z_at, 8)) for k in range(1, n)]
    for to in peers:
        pl.semaphore_signal(barrier, inc=1, device_id=to, device_id_type=MESH)
    p_own[...] = jnp.zeros(p_own.shape, F32)

    def combine(i, yy):
        cc = pairs[i][0]
        cols = pl.ds(pl.multiple_of(yy % 2 * WIDTH, 128), WIDTH)
        comb[cc, yy] = g_buf[i, :, cols].astype(F32) + f_buf[i, :, cols]

    def to_core(name, yy):
        send(name, comb.at[1 - c, yy], c_recv.at[yy], core_peer)
        net.expect(name, c_recv.at[yy], core_peer)

    def sum_cores(name, yy):
        take(name)
        s_buf[yy] = comb[c, yy] + c_recv[yy]

    def left_product(i, yy):
        hi, lo = split(comb[pairs[i][0], yy])
        cols = pl.ds(pl.multiple_of((2 * pairs[i][0] + yy % 2) * WIDTH, 128), WIDTH)
        right = jnp.concatenate(split(r_buf[yy // 2, :, cols]), axis=0)
        both = (dot(hi, right, ((1,), (1,))) + dot(lo, right, ((1,), (1,)))).T
        p_own[yy // 2, :, 0:ROWS] += both[:RANK] + both[RANK:]

    y_beside = mat * 2 + 1 - y % 2
    y_across = (1 - mat) * 2 + 1 - y % 2
    order = [(0, y_far), (1, y_far), (0, y_across), (1, y_across), (2, y_beside), (3, y_beside), (2, y), (3, y)]
    top, low = pl.ds(0, HALF), pl.ds(HALF, HALF)

    def wait_load(i):
        for copy in loads[i]:
            copy.wait()

    wait_load(0)
    combine(0, y_far)
    pl.semaphore_wait(barrier, len(peers))
    to_core("c_far", y_far)
    combine(0, y_across)
    to_core("c_across", y_across)
    wait_load(1)
    combine(1, y_far)
    combine(1, y_across)
    wait_load(2)
    combine(2, y_beside)
    to_core("c_beside", y_beside)
    combine(2, y)
    to_core("c_own", y)
    right_load.wait()
    for step in order[:3]:
        left_product(*step)
    sum_cores("c_far", y_far)
    send("r_top", s_buf.at[y_far, top], r1.at[0], y_at(1))
    send("r_low", s_buf.at[y_far, low], r1.at[1], y_at(3))
    net.expect("r_top", r1.at[0], y_at(1))
    net.expect("r_low", r1.at[1], y_at(3))
    wait_load(3)
    combine(3, y_beside)
    combine(3, y)
    for step in order[3:]:
        left_product(*step)

    ranks = pl.ds(pl.multiple_of(c * 16, 16), 16)
    send("p_core", p_own, p_core, core_peer)
    net.expect("p_core", p_core, core_peer)
    sum_cores("c_across", y_across)
    sum_cores("c_beside", y_beside)
    take("p_core")
    p_mid[...] = p_own[...] + p_core[...]
    for k in (2, 1, 3):
        send("p_y", p_mid.at[(y + k) % 4 // 2, ranks], p_y.at[y], y_at(k))
    net.expect("p_y", p_y.at[pl.ds(0, 3)], core_peer)
    p_y[y] = p_mid[mat, ranks]

    send("r_end", s_buf.at[y_next, low], r2.at[0], y_at(1))
    send("r_end", s_buf.at[y_prev, top], r2.at[1], y_at(3))
    net.expect("r_end", r2, core_peer)
    take("r_top")
    s_buf[y_next, top] += r1[0]
    send("r_end", s_buf.at[y_next, top], r2.at[2], y_at(1))
    take("r_low")
    s_buf[y_prev, low] += r1[1]
    send("r_end", s_buf.at[y_prev, low], r2.at[3], y_at(3))
    sum_cores("c_own", y)

    take("p_y")
    p_x[x] = tree_sum([p_y[i] for i in range(4)])
    for k in (2, 1, 3):
        send("p_x", p_x.at[x], p_x.at[x], x_at(k))
    net.expect("p_x", p_x.at[pl.ds(0, 3)], core_peer)
    take("p_x")
    p_z[z] = tree_sum([p_x[i] for i in range(4)])
    for k in (4, 3, 5, 2, 6, 1, 7):
        send("p_z", p_z.at[z], p_z.at[z], z_at(k))
    net.expect("p_z", p_z.at[pl.ds(0, 7)], core_peer)
    take("p_z")
    p_full[ranks] = tree_sum([p_z[i] for i in range(8)]) * (1.0 / REPLICAS)
    send("p_full", p_full.at[ranks], p_full.at[ranks], core_peer)
    net.expect("p_full", p_full.at[pl.ds(pl.multiple_of(16 - c * 16, 16), 16)], core_peer)
    take("p_full")
    take("r_end")
    s_buf[y, top] = (s_buf[y, top] + r2[1]) + r2[2]
    s_buf[y, low] = (s_buf[y, low] + r2[0]) + r2[3]

    near = zl // 2
    far = 1 - near
    owner = (zl == 1) | (zl == 2)

    def cols_of(piece):
        return pl.ds(*PIECES[piece])

    def to_owner(h, piece):
        cols = cols_of(piece)
        return net.copy("z_sum%d" % piece, q_part.at[h, :, cols], z_part.at[zl, :, cols], at(zl_=1 + h))

    def from_owner(h, k, piece):
        mine = q_all.at[c, y, h, :, cols_of(piece)]
        return net.copy("half%d%d" % (h, piece), mine, mine, zl_at(k))

    left = jnp.concatenate(split(p_full[:, :ROWS]), axis=0)
    for piece in range(2):
        cols = cols_of(piece)
        hi, lo = split(s_buf[y, :, cols])
        prod = dot(left, hi, ((1,), (0,))) + dot(left, lo, ((1,), (0,)))
        q_part[:, :, cols] = (prod[:RANK] + prod[RANK:]).reshape(2, 16, PIECES[piece][1])
        for h in range(2):
            pl.when(zl != 1 + h)(to_owner(h, piece).start)

    @net.at_end
    def _():
        for piece in range(2):
            for h in range(2):
                pl.when(zl != 1 + h)(to_owner(h, piece).wait_send)

        @pl.when(owner)
        def _():
            for piece in range(2):
                for k in (1, 2, 3):
                    from_owner(0, k, piece).wait_send()

    w_t[mat, :, 0:ROWS] = left_times_inverse(p_full[:, :ROWS]) * (1.0 / REPLICAS)
    send("w", w_t.at[mat], w_t.at[mat], y_at(2))
    net.expect("w", w_t.at[1 - mat], y_at(2))

    def hand_on(tag, yy, half, piece, to):
        part = q_all.at[c, yy, half, :, cols_of(piece)]
        send(tag, part, part, to)

    for half, name in ((near, "near"), (far, "far")):
        for piece in range(2):
            cols = cols_of(piece)
            landing = [net.landing("half%d%d" % (h, piece), q_all.at[c, y, h, :, cols], core_peer) for h in range(2)]

            def land(half=half, landing=landing):
                for h in range(2):
                    pl.when(half == h)(landing[h])

            if name == "far":
                land()
            else:

                @pl.when(owner)
                def _(piece=piece, cols=cols):
                    z_part[zl, :, cols] = q_part[near, :, cols]
                    net.landing("z_sum%d" % piece, z_part.at[pl.ds(0, 3), :, cols], core_peer)()
                    q_all[c, y, near, :, cols] = tree_sum([z_part[i, :, cols] for i in range(4)])
                    for h in range(2):

                        @pl.when(near == h)
                        def _():
                            for k in (1, 2, 3):
                                from_owner(h, k, piece).start()

                pl.when(jnp.logical_not(owner))(land)
            for k in (2, 1, 3):
                tag = "%s%d_%d" % (name, piece, k)
                hand_on(tag, y, half, piece, y_at(k))
                net.expect(tag, q_all.at[c, (y + 4 - k) % 4, half, :, cols], core_peer)
            hand_on("core", y, half, piece, core_peer)
    net.expect("core", q_all.at[1 - c], core_peer)

    def decode_own(yy):
        out = decode(w_out[yy // 2], q_all[c, yy].reshape(RANK, WIDTH))
        decoded[yy] = out
        carried[yy] = comb[c, yy] - out

    for half, name in ((near, "near"), (far, "far")):
        for piece in range(2):
            for k in (1, 3, 2):
                take("%s%d_%d" % (name, piece, k))
                hand_on("core", (y + 4 - k) % 4, half, piece, core_peer)
        if name == "near":
            take("w")
            for i in range(MATS):
                hi, lo = split(w_t[i, :, 0:ROWS].T)
                w_out[i] = jnp.concatenate([hi, lo, hi, lo], axis=1)
            decode_own(y)
    for k in (1, 3, 2):
        decode_own((y + 4 - k) % 4)
    net.finish()


def write_kernel(comb, q_all, w_ref, own_decoded, own_carried, decoded, carried, d_buf, c_buf, sem):
    c = lax.axis_index("dp") % 2
    copies = []

    def write(cc, yy, d_ref, c_ref):
        cols = pl.ds(pl.multiple_of((2 * cc + yy % 2) * WIDTH, 128), WIDTH)
        for ref, to in ((d_ref, decoded.at[yy // 2, :, cols]), (c_ref, carried.at[0, yy // 2, :, cols])):
            copies.append(pltpu.make_async_copy(ref, to, sem.at[0]))
            copies[-1].start()

    for yy in range(4):
        write(c, yy, own_decoded.at[yy], own_carried.at[yy])
    for yy in range(4):
        out = decode(w_ref[yy // 2], q_all[1 - c, yy].reshape(RANK, WIDTH))
        d_buf[yy] = out
        c_buf[yy] = comb[1 - c, yy] - out
        write(1 - c, yy, d_buf.at[yy], c_buf.at[yy])
    for copy in copies:
        copy.wait()


def reduce_call(gradient, feedback, right_initial, name="reduce", collective_id=0):
    right_t = jnp.swapaxes(right_initial, 1, 2)
    vmem = pl.BlockSpec(memory_space=pltpu.VMEM)
    hbm = pl.BlockSpec(memory_space=pltpu.HBM)
    dma = pltpu.SemaphoreType.DMA
    return pl.pallas_call(
        reduce_kernel,
        name=name,
        out_shape=(
            jax.ShapeDtypeStruct((2, 4, ROWS, WIDTH), F32),
            jax.ShapeDtypeStruct((2, 4, 2, 16, WIDTH), F32),
            jax.ShapeDtypeStruct((MATS, ROWS, 128), BF16),
            jax.ShapeDtypeStruct((4, ROWS, WIDTH), F32),
            jax.ShapeDtypeStruct((4, ROWS, WIDTH), F32),
        ),
        in_specs=[hbm] * 3,
        out_specs=(vmem,) * 5,
        scratch_shapes=[
            pltpu.VMEM((4, ROWS, 2 * WIDTH), BF16),
            pltpu.VMEM((4, ROWS, 2 * WIDTH), F32),
            pltpu.VMEM((MATS, RANK, COLS), F32),
            pltpu.VMEM((4, ROWS, WIDTH), F32),
            pltpu.VMEM((4, ROWS, WIDTH), F32),
            pltpu.VMEM((2, HALF, WIDTH), F32),
            pltpu.VMEM((4, HALF, WIDTH), F32),
            pltpu.VMEM((MATS, RANK, 128), F32),
            pltpu.VMEM((MATS, RANK, 128), F32),
            pltpu.VMEM((MATS, RANK, 128), F32),
            pltpu.VMEM((4, 16, 128), F32),
            pltpu.VMEM((4, 16, 128), F32),
            pltpu.VMEM((8, 16, 128), F32),
            pltpu.VMEM((RANK, 128), F32),
            pltpu.VMEM((MATS, RANK, 128), F32),
            pltpu.VMEM((2, 16, WIDTH), F32),
            pltpu.VMEM((4, 16, WIDTH), F32),
            dma((9,)),
            dma((1,)),
            dma((TAGS,)),
        ],
        compiler_params=pltpu.CompilerParams(
            collective_id=collective_id, has_side_effects=True, vmem_limit_bytes=VMEM_BYTES
        ),
    )(*(pltpu.with_memory_space_constraint(a, pltpu.HBM) for a in (gradient, feedback, right_t)))


def per_device(gradient, feedback, right_initial):
    vmem = pl.BlockSpec(memory_space=pltpu.VMEM)
    hbm = pl.BlockSpec(memory_space=pltpu.HBM)
    return pl.pallas_call(
        write_kernel,
        name="write",
        out_shape=(
            jax.ShapeDtypeStruct((MATS, ROWS, COLS), F32),
            jax.ShapeDtypeStruct((1, MATS, ROWS, COLS), F32),
        ),
        in_specs=[vmem] * 5,
        out_specs=(hbm, hbm),
        scratch_shapes=[
            pltpu.VMEM((4, ROWS, WIDTH), F32),
            pltpu.VMEM((4, ROWS, WIDTH), F32),
            pltpu.SemaphoreType.DMA((1,)),
        ],
        compiler_params=pltpu.CompilerParams(vmem_limit_bytes=VMEM_BYTES),
    )(*reduce_call(gradient, feedback, right_initial))


def solution(mesh):
    placed = (P("dp", None, None, "mp"), P("dp", None, None, "mp"), P(None, "mp", None))
    return jax.shard_map(
        per_device,
        mesh=mesh,
        in_specs=placed,
        out_specs=(P(None, None, "mp"), P("dp", None, None, "mp")),
        check_vma=False,
    )
```

```python
import jax
import jax.numpy as jnp
from jax import lax
from jax.experimental import pallas as pl
from jax.experimental.pallas import tpu as pltpu
from jax.sharding import PartitionSpec as P

MESH = pl.DeviceIdType.MESH
F32 = jnp.float32
BF16 = jnp.bfloat16
MATS, ROWS, RANK, COLS = 2, 96, 32, 3584
WIDTH = 896
PIECES = ((0, 256), (256, 256), (512, 256), (768, 128))
HALF = ROWS // 2
REPLICAS = 32
TAGS = 56
VMEM_BYTES = 32 << 20


def split(a):
    hi = a.astype(BF16)
    return hi, (a - hi.astype(F32)).astype(BF16)


def dot(a, b, contract):
    return lax.dot_general(a, b, ((contract[0], contract[1]), ((), ())), preferred_element_type=F32)


def exact(a, b, contract):
    return lax.dot_general(
        a, b, ((contract[0], contract[1]), ((), ())), precision=lax.Precision.HIGHEST, preferred_element_type=F32
    )


def left_times_inverse(p_t):
    gram = exact(p_t, p_t, ((1,), (1,)))
    row = lax.broadcasted_iota(jnp.int32, (RANK, RANK), 0)
    col = lax.broadcasted_iota(jnp.int32, (RANK, RANK), 1)
    eye = jnp.where(row == col, 1.0, 0.0).astype(F32)
    inv = eye
    for k in range(RANK - 1):
        scale = 1.0 / gram[k : k + 1, k : k + 1]
        factor = jnp.where(row > k, jnp.broadcast_to(gram[:, k : k + 1], (RANK, RANK)), 0.0)
        gram, inv = (a - factor * (a[k : k + 1, :] * scale) for a in (gram, inv))
    diag = jnp.sum(gram * eye, axis=1, keepdims=True)
    l_inv = inv * lax.rsqrt(diag)
    orth_t = exact(l_inv, p_t, ((1,), (0,)))
    return exact(l_inv, orth_t, ((0,), (0,)))


def decode(left, q):
    hi, lo = split(q)
    return dot(left, jnp.concatenate([hi, hi, lo, lo], axis=0), ((1,), (0,)))


class Net:
    def __init__(self, send_sem, recv_sem):
        self.send_sem, self.recv_sem = send_sem, recv_sem
        self.tags, self.due, self.sent, self.last = {}, {}, [], []

    def copy(self, tag, src, dst, to):
        return pltpu.make_async_remote_copy(
            src_ref=src,
            dst_ref=dst,
            send_sem=self.send_sem.at[0],
            recv_sem=self.recv_sem.at[self.tags.setdefault(tag, len(self.tags))],
            device_id=to,
            device_id_type=MESH,
        )

    def send(self, tag, src, dst, to):
        self.sent.append(self.copy(tag, src, dst, to))
        self.sent[-1].start()

    def landing(self, tag, ref, to):
        return self.copy(tag, ref, ref, to).wait_recv

    def expect(self, tag, ref, to):
        self.due[tag] = self.landing(tag, ref, to)

    def take(self, tag):
        self.due.pop(tag)()

    def at_end(self, step):
        self.last.append(step)

    def finish(self):
        for tag in list(self.due):
            self.take(tag)
        for copy in self.sent:
            copy.wait_send()
        for step in self.last:
            step()


def tree_sum(terms):
    while len(terms) > 1:
        terms = [a + b for a, b in zip(terms[::2], terms[1::2])]
    return terms[0]


def reduce_kernel(
    g_hbm, f_hbm, r_hbm, comb, q_all, w_out, decoded, carried,
    g_buf, f_buf, r_buf, c_recv, s_buf, r1, r2, p_own, p_y, p_x, p_z, p_full, w_t, q_part, z_part,
    load_sem, send_sem, recv_sem,
):
    d = lax.axis_index("dp")
    m = lax.axis_index("mp")
    zl, y, c = d // 8, (d // 2) % 4, d % 2
    x, zh = m // 2, m % 2
    z = zh * 4 + zl
    net = Net(send_sem, recv_sem)
    send, take = net.send, net.take

    def at(zl_=zl, y_=y, c_=c, x_=x, zh_=zh):
        return (zl_ * 8 + y_ * 2 + c_, x_ * 2 + zh_)

    def y_at(k):
        return at(y_=(y + k) % 4)

    def x_at(k):
        return at(x_=(x + k) % 4)

    def z_at(k):
        to = (z + k) % 8
        return at(zl_=to % 4, zh_=to // 4)

    def zl_at(k):
        return at(zl_=(zl + k) % 4)

    core_peer = at(c_=1 - c)
    y_next, y_prev, y_far = (y + 1) % 4, (y + 3) % 4, (y + 2) % 4
    mat = y // 2

    pairs = [(1 - c, 1 - mat), (c, 1 - mat), (1 - c, mat), (c, mat)]
    loads = []
    for i, (cc, mm) in enumerate(pairs):
        cols = pl.ds(pl.multiple_of(cc * 2 * WIDTH, 128), 2 * WIDTH)
        loads.append(
            (
                pltpu.make_async_copy(f_hbm.at[0, mm, :, cols], f_buf.at[i], load_sem.at[i]),
                pltpu.make_async_copy(g_hbm.at[0, mm, :, cols], g_buf.at[i], load_sem.at[4 + i]),
            )
        )
    right_load = pltpu.make_async_copy(r_hbm, r_buf, load_sem.at[8])
    right_load.start()
    for copies in loads:
        for copy in copies:
            copy.start()

    barrier = pltpu.get_barrier_semaphore()
    peers = [core_peer] + [at(y_=(y + k) % 4, c_=1 - c) for k in (1, 2, 3)] + [f(k) for f, n in ((y_at, 4), (x_at, 4), (z_at, 8)) for k in range(1, n)]
    for to in peers:
        pl.semaphore_signal(barrier, inc=1, device_id=to, device_id_type=MESH)
    p_own[...] = jnp.zeros(p_own.shape, F32)
    p_sums = {}

    def combine(i, yy):
        cc = pairs[i][0]
        cols = pl.ds(pl.multiple_of(yy % 2 * WIDTH, 128), WIDTH)
        comb[cc, yy] = g_buf[i, :, cols].astype(F32) + f_buf[i, :, cols]

    def to_core(name, yy):
        send(name, comb.at[1 - c, yy], c_recv.at[yy], core_peer)
        net.expect(name, c_recv.at[yy], core_peer)

    def sum_cores(name, yy):
        take(name)
        s_buf[yy] = comb[c, yy] + c_recv[yy]

    def left_product(i, yy):
        hi, lo = split(comb[pairs[i][0], yy])
        cols = pl.ds(pl.multiple_of((2 * pairs[i][0] + yy % 2) * WIDTH, 128), WIDTH)
        right = jnp.concatenate(split(r_buf[yy // 2, :, cols]), axis=0)
        both = dot(jnp.concatenate([hi, lo], axis=0), right, ((1,), (1,)))
        p_sums.setdefault(i // 2, []).append(both[:ROWS] + both[ROWS:])

    def left_sum(i):
        both = tree_sum(p_sums[i]).T
        p_own[mat if i else 1 - mat, :, 0:ROWS] = both[:RANK] + both[RANK:]

    y_beside = mat * 2 + 1 - y % 2
    y_across = (1 - mat) * 2 + 1 - y % 2
    top, low = pl.ds(0, HALF), pl.ds(HALF, HALF)

    def wait_load(i):
        for copy in loads[i]:
            copy.wait()

    right_load.wait()
    for i in range(4):
        wait_load(i)
        if i == 0:
            pl.semaphore_wait(barrier, len(peers))
        for name, yy in ((("far", y_far), ("across", y_across)), (("beside", y_beside), ("own", y)))[i // 2]:
            combine(i, yy)
            if i % 2 == 0:
                to_core("c_" + name, yy)
            left_product(i, yy)
        if i % 2 == 1:
            left_sum(i // 2)

    ranks = pl.ds(pl.multiple_of(c * 16, 16), 16)
    for k in (2, 1, 3, 0):
        for same in ((0, 1) if k else (0,)):
            cc = c if same else 1 - c
            part = p_own.at[(y + k) % 4 // 2, pl.ds(pl.multiple_of(cc * 16, 16), 16)]
            send("p_y", part, p_y.at[2 * y + c], at(y_=(y + k) % 4, c_=cc))
    net.expect("p_y", p_y.at[pl.ds(0, 7)], core_peer)
    p_y[2 * y + c] = p_own[mat, ranks]

    sum_cores("c_far", y_far)
    send("r_top", s_buf.at[y_far, top], r1.at[0], y_at(1))
    send("r_low", s_buf.at[y_far, low], r1.at[1], y_at(3))
    net.expect("r_top", r1.at[0], y_at(1))
    net.expect("r_low", r1.at[1], y_at(3))
    sum_cores("c_across", y_across)
    sum_cores("c_beside", y_beside)
    sum_cores("c_own", y)

    take("p_y")
    p_x[x] = tree_sum([p_y[i] for i in range(8)])
    for k in (2, 1, 3):
        send("p_x", p_x.at[x], p_x.at[x], x_at(k))
    net.expect("p_x", p_x.at[pl.ds(0, 3)], core_peer)
    send("r_end", s_buf.at[y_next, low], r2.at[0], y_at(1))
    send("r_end", s_buf.at[y_prev, top], r2.at[1], y_at(3))
    net.expect("r_end", r2, core_peer)
    take("r_top")
    s_buf[y_next, top] += r1[0]
    send("r_end", s_buf.at[y_next, top], r2.at[2], y_at(1))
    take("r_low")
    s_buf[y_prev, low] += r1[1]
    send("r_end", s_buf.at[y_prev, low], r2.at[3], y_at(3))

    take("p_x")
    p_z[z] = tree_sum([p_x[i] for i in range(4)])
    for k in (4, 3, 5, 2, 6, 1, 7):
        send("p_z", p_z.at[z], p_z.at[z], z_at(k))
    net.expect("p_z", p_z.at[pl.ds(0, 7)], core_peer)
    take("p_z")
    p_full[ranks] = tree_sum([p_z[i] for i in range(8)]) * (1.0 / REPLICAS)
    send("p_full", p_full.at[ranks], p_full.at[ranks], core_peer)
    net.expect("p_full", p_full.at[pl.ds(pl.multiple_of(16 - c * 16, 16), 16)], core_peer)
    take("p_full")
    take("r_end")
    s_buf[y, top] = (s_buf[y, top] + r2[1]) + r2[2]
    s_buf[y, low] = (s_buf[y, low] + r2[0]) + r2[3]

    near = zl // 2
    far = 1 - near
    owner = (zl == 1) | (zl == 2)

    def cols_of(piece):
        return pl.ds(*PIECES[piece])

    def to_owner(h, piece):
        cols = cols_of(piece)
        return net.copy("z_sum%d" % piece, q_part.at[h, :, cols], z_part.at[zl, :, cols], at(zl_=1 + h))

    def from_owner(h, k, piece):
        mine = q_all.at[c, y, h, :, cols_of(piece)]
        return net.copy("half%d%d" % (h, piece), mine, mine, zl_at(k))

    left = jnp.concatenate(split(p_full[:, :ROWS]), axis=0)
    for piece in range(len(PIECES)):
        cols = cols_of(piece)
        hi, lo = split(s_buf[y, :, cols])
        prod = dot(left, hi, ((1,), (0,))) + dot(left, lo, ((1,), (0,)))
        q_part[:, :, cols] = (prod[:RANK] + prod[RANK:]).reshape(2, 16, PIECES[piece][1])
        for h in range(2):
            pl.when(zl != 1 + h)(to_owner(h, piece).start)

    @net.at_end
    def _():
        for piece in range(len(PIECES)):
            for h in range(2):
                pl.when(zl != 1 + h)(to_owner(h, piece).wait_send)

        @pl.when(owner)
        def _():
            for piece in range(len(PIECES)):
                for k in (1, 2, 3):
                    from_owner(0, k, piece).wait_send()

    w_t[mat, :, 0:ROWS] = left_times_inverse(p_full[:, :ROWS]) * (1.0 / REPLICAS)
    send("w", w_t.at[mat], w_t.at[mat], y_at(2))
    net.expect("w", w_t.at[1 - mat], y_at(2))

    def hand_on(tag, yy, half, piece, to):
        part = q_all.at[c, yy, half, :, cols_of(piece)]
        send(tag, part, part, to)

    for half, name in ((near, "near"), (far, "far")):
        for piece in range(len(PIECES)):
            cols = cols_of(piece)
            landing = [net.landing("half%d%d" % (h, piece), q_all.at[c, y, h, :, cols], core_peer) for h in range(2)]

            def land(half=half, landing=landing):
                for h in range(2):
                    pl.when(half == h)(landing[h])

            if name == "far":
                land()
            else:

                @pl.when(owner)
                def _(piece=piece, cols=cols):
                    z_part[zl, :, cols] = q_part[near, :, cols]
                    net.landing("z_sum%d" % piece, z_part.at[pl.ds(0, 3), :, cols], core_peer)()
                    q_all[c, y, near, :, cols] = tree_sum([z_part[i, :, cols] for i in range(4)])
                    for h in range(2):

                        @pl.when(near == h)
                        def _():
                            for k in (1, 2, 3):
                                from_owner(h, k, piece).start()

                pl.when(jnp.logical_not(owner))(land)
            for k in (2, 1, 3):
                tag = "%s%d_%d" % (name, piece, k)
                hand_on(tag, y, half, piece, y_at(k))
                net.expect(tag, q_all.at[c, (y + 4 - k) % 4, half, :, cols], core_peer)
            hand_on("core", y, half, piece, core_peer)
    net.expect("core", q_all.at[1 - c], core_peer)

    def decode_own(yy):
        out = decode(w_out[yy // 2], q_all[c, yy].reshape(RANK, WIDTH))
        decoded[yy] = out
        carried[yy] = comb[c, yy] - out

    for half, name in ((near, "near"), (far, "far")):
        for piece in range(len(PIECES)):
            for k in (1, 3, 2):
                take("%s%d_%d" % (name, piece, k))
                hand_on("core", (y + 4 - k) % 4, half, piece, core_peer)
        if name == "near":
            take("w")
            for i in range(MATS):
                hi, lo = split(w_t[i, :, 0:ROWS].T)
                w_out[i] = jnp.concatenate([hi, lo, hi, lo], axis=1)
            decode_own(y)
    for k in (1, 3, 2):
        decode_own((y + 4 - k) % 4)
    net.finish()


def write_kernel(comb, q_all, w_ref, own_decoded, own_carried, decoded, carried, d_buf, c_buf, sem):
    c = lax.axis_index("dp") % 2
    copies = []

    def write(cc, yy, d_ref, c_ref):
        cols = pl.ds(pl.multiple_of((2 * cc + yy % 2) * WIDTH, 128), WIDTH)
        for ref, to in ((d_ref, decoded.at[yy // 2, :, cols]), (c_ref, carried.at[0, yy // 2, :, cols])):
            copies.append(pltpu.make_async_copy(ref, to, sem.at[0]))
            copies[-1].start()

    for yy in range(4):
        write(c, yy, own_decoded.at[yy], own_carried.at[yy])
    for yy in range(4):
        out = decode(w_ref[yy // 2], q_all[1 - c, yy].reshape(RANK, WIDTH))
        d_buf[yy] = out
        c_buf[yy] = comb[1 - c, yy] - out
        write(1 - c, yy, d_buf.at[yy], c_buf.at[yy])
    for copy in copies:
        copy.wait()


def reduce_call(gradient, feedback, right_initial, name="reduce", collective_id=0):
    right_t = jnp.swapaxes(right_initial, 1, 2)
    vmem = pl.BlockSpec(memory_space=pltpu.VMEM)
    hbm = pl.BlockSpec(memory_space=pltpu.HBM)
    dma = pltpu.SemaphoreType.DMA
    return pl.pallas_call(
        reduce_kernel,
        name=name,
        out_shape=(
            jax.ShapeDtypeStruct((2, 4, ROWS, WIDTH), F32),
            jax.ShapeDtypeStruct((2, 4, 2, 16, WIDTH), F32),
            jax.ShapeDtypeStruct((MATS, ROWS, 128), BF16),
            jax.ShapeDtypeStruct((4, ROWS, WIDTH), F32),
            jax.ShapeDtypeStruct((4, ROWS, WIDTH), F32),
        ),
        in_specs=[hbm] * 3,
        out_specs=(vmem,) * 5,
        scratch_shapes=[
            pltpu.VMEM((4, ROWS, 2 * WIDTH), BF16),
            pltpu.VMEM((4, ROWS, 2 * WIDTH), F32),
            pltpu.VMEM((MATS, RANK, COLS), F32),
            pltpu.VMEM((4, ROWS, WIDTH), F32),
            pltpu.VMEM((4, ROWS, WIDTH), F32),
            pltpu.VMEM((2, HALF, WIDTH), F32),
            pltpu.VMEM((4, HALF, WIDTH), F32),
            pltpu.VMEM((MATS, RANK, 128), F32),
            pltpu.VMEM((8, 16, 128), F32),
            pltpu.VMEM((4, 16, 128), F32),
            pltpu.VMEM((8, 16, 128), F32),
            pltpu.VMEM((RANK, 128), F32),
            pltpu.VMEM((MATS, RANK, 128), F32),
            pltpu.VMEM((2, 16, WIDTH), F32),
            pltpu.VMEM((4, 16, WIDTH), F32),
            dma((9,)),
            dma((1,)),
            dma((TAGS,)),
        ],
        compiler_params=pltpu.CompilerParams(
            collective_id=collective_id, has_side_effects=True, vmem_limit_bytes=VMEM_BYTES
        ),
    )(*(pltpu.with_memory_space_constraint(a, pltpu.HBM) for a in (gradient, feedback, right_t)))


def per_device(gradient, feedback, right_initial):
    vmem = pl.BlockSpec(memory_space=pltpu.VMEM)
    hbm = pl.BlockSpec(memory_space=pltpu.HBM)
    return pl.pallas_call(
        write_kernel,
        name="write",
        out_shape=(
            jax.ShapeDtypeStruct((MATS, ROWS, COLS), F32),
            jax.ShapeDtypeStruct((1, MATS, ROWS, COLS), F32),
        ),
        in_specs=[vmem] * 5,
        out_specs=(hbm, hbm),
        scratch_shapes=[
            pltpu.VMEM((4, ROWS, WIDTH), F32),
            pltpu.VMEM((4, ROWS, WIDTH), F32),
            pltpu.SemaphoreType.DMA((1,)),
        ],
        compiler_params=pltpu.CompilerParams(vmem_limit_bytes=VMEM_BYTES),
    )(*reduce_call(gradient, feedback, right_initial))


def solution(mesh):
    placed = (P("dp", None, None, "mp"), P("dp", None, None, "mp"), P(None, "mp", None))
    return jax.shard_map(
        per_device,
        mesh=mesh,
        in_specs=placed,
        out_specs=(P(None, None, "mp"), P("dp", None, None, "mp")),
        check_vma=False,
    )
```

```python
import jax
import jax.numpy as jnp
from jax import lax
from jax.experimental import pallas as pl
from jax.experimental.pallas import tpu as pltpu
from jax.sharding import PartitionSpec as P

MESH = pl.DeviceIdType.MESH
F32 = jnp.float32
BF16 = jnp.bfloat16
MATS, ROWS, RANK, COLS = 2, 96, 32, 3584
WIDTH = 896
PIECES = ((0, 384), (384, 256), (640, 256))
RING = (pl.ds(0, 640), pl.ds(640, 256))
HALF = ROWS // 2
REPLICAS = 32
BLOCK = 4
TAGS = 36
VMEM_BYTES = 32 << 20


def split(a):
    hi = a.astype(BF16)
    return hi, (a - hi.astype(F32)).astype(BF16)


def dot(a, b, contract):
    return lax.dot_general(a, b, ((contract[0], contract[1]), ((), ())), preferred_element_type=F32)


def exact(a, b, contract):
    return lax.dot_general(
        a, b, ((contract[0], contract[1]), ((), ())), precision=lax.Precision.HIGHEST, preferred_element_type=F32
    )


def left_times_inverse(p_t):
    gram = exact(p_t, p_t, ((1,), (1,)))
    row = lax.broadcasted_iota(jnp.int32, (RANK, RANK), 0)
    col = lax.broadcasted_iota(jnp.int32, (RANK, RANK), 1)
    eye = jnp.where(row == col, 1.0, 0.0).astype(F32)
    inv = eye
    for start in range(0, RANK, BLOCK):
        columns = [jnp.broadcast_to(gram[:, k : k + 1], (RANK, RANK)) for k in range(start, start + BLOCK)]
        for j, k in enumerate(range(start, start + BLOCK)):
            factor = jnp.where(row > k, columns[j] * (1.0 / columns[j][k : k + 1, :]), 0.0)
            gram, inv = (a - factor * a[k : k + 1, :] for a in (gram, inv))
            columns[j + 1 :] = [a - factor * a[k : k + 1, :] for a in columns[j + 1 :]]
    diag = jnp.sum(gram * eye, axis=1, keepdims=True)
    l_inv = inv * lax.rsqrt(diag)
    orth_t = exact(l_inv, p_t, ((1,), (0,)))
    return exact(l_inv, orth_t, ((0,), (0,)))


def decode(left, q):
    hi, lo = split(q)
    return dot(left, jnp.concatenate([hi, hi, lo, lo], axis=0), ((1,), (0,)))


class Net:
    def __init__(self, send_sem, recv_sem):
        self.send_sem, self.recv_sem = send_sem, recv_sem
        self.tags, self.due, self.last = {"": 0}, {}, []

    def copy(self, tag, src, dst, to):
        return pltpu.make_async_remote_copy(
            src_ref=src,
            dst_ref=dst,
            send_sem=self.send_sem.at[0],
            recv_sem=self.recv_sem.at[self.tags.setdefault(tag, len(self.tags))],
            device_id=to,
            device_id_type=MESH,
        )

    def send(self, tag, src, dst, to):
        self.copy(tag, src, dst, to).start()

    def landing(self, tag, ref, to):
        return self.copy(tag, ref, ref, to).wait_recv

    def expect(self, tag, ref, to):
        self.due[tag] = self.landing(tag, ref, to)

    def take(self, tag):
        self.due.pop(tag)()

    def at_end(self, step):
        self.last.append(step)

    def finish(self, totals, to):
        for tag in list(self.due):
            self.take(tag)
        for ref in totals:
            self.copy("", ref, ref, to).wait_send()
        for step in self.last:
            step()


def tree_sum(terms):
    while len(terms) > 1:
        terms = [a + b for a, b in zip(terms[::2], terms[1::2])]
    return terms[0]


def reduce_kernel(
    g_hbm, f_hbm, r_hbm, comb, q_all, w_out, decoded, carried,
    g_buf, f_buf, r_buf, c_recv, s_buf, r1, r2, p_own, p_y, p_x, p_z, p_full, w_t, q_part, z_part,
    load_sem, send_sem, recv_sem,
):
    d = lax.axis_index("dp")
    m = lax.axis_index("mp")
    zl, y, c = d // 8, (d // 2) % 4, d % 2
    x, zh = m // 2, m % 2
    z = zh * 4 + zl
    net = Net(send_sem, recv_sem)
    send, take = net.send, net.take

    def at(zl_=zl, y_=y, c_=c, x_=x, zh_=zh):
        return (zl_ * 8 + y_ * 2 + c_, x_ * 2 + zh_)

    def y_at(k):
        return at(y_=(y + k) % 4)

    def x_at(k):
        return at(x_=(x + k) % 4)

    def z_at(k):
        to = (z + k) % 8
        return at(zl_=to % 4, zh_=to // 4)

    def zl_at(k):
        return at(zl_=(zl + k) % 4)

    core_peer = at(c_=1 - c)
    y_next, y_prev, y_far = (y + 1) % 4, (y + 3) % 4, (y + 2) % 4
    mat = y // 2

    barrier = pltpu.get_barrier_semaphore()

    def greet(peers):
        for to in peers:
            pl.semaphore_signal(barrier, inc=1, device_id=to, device_id_type=MESH)

    z_peers = [z_at(k) for k in (4, 3, 5, 2, 6, 1, 7)]
    greet(z_peers)

    pairs = [(1 - c, 1 - mat), (c, 1 - mat), (1 - c, mat), (c, mat)]
    loads = []
    for i, (cc, mm) in enumerate(pairs):
        cols = pl.ds(pl.multiple_of(cc * 2 * WIDTH, 128), 2 * WIDTH)
        loads.append(
            (
                pltpu.make_async_copy(f_hbm.at[0, mm, :, cols], f_buf.at[i], load_sem.at[i]),
                pltpu.make_async_copy(g_hbm.at[0, mm, :, cols], g_buf.at[i], load_sem.at[i]),
            )
        )
    right_load = pltpu.make_async_copy(r_hbm, r_buf, load_sem.at[4])
    right_load.start()
    for copies in loads:
        for copy in copies:
            copy.start()

    near_peers = [core_peer] + [at(y_=(y + k) % 4, c_=cc) for k in (2, 1, 3) for cc in (c, 1 - c)]
    near_peers += [x_at(k) for k in (2, 1, 3)]
    greet(near_peers)
    p_own[...] = jnp.zeros(p_own.shape, F32)
    p_sums = {}

    def combine(i, yy):
        cc = pairs[i][0]
        cols = pl.ds(pl.multiple_of(yy % 2 * WIDTH, 128), WIDTH)
        comb[cc, yy] = g_buf[i, :, cols].astype(F32) + f_buf[i, :, cols]

    def to_core(name, yy):
        send(name, comb.at[1 - c, yy], c_recv.at[yy], core_peer)
        net.expect(name, c_recv.at[yy], core_peer)

    def sum_cores(name, yy):
        take(name)
        s_buf[yy] = comb[c, yy] + c_recv[yy]

    def left_product(i, yy):
        hi, lo = split(comb[pairs[i][0], yy])
        cols = pl.ds(pl.multiple_of((2 * pairs[i][0] + yy % 2) * WIDTH, 128), WIDTH)
        right = jnp.concatenate(split(r_buf[yy // 2, :, cols]), axis=0)
        both = dot(jnp.concatenate([hi, lo], axis=0), right, ((1,), (1,)))
        p_sums.setdefault(i // 2, []).append(both[:ROWS] + both[ROWS:])

    def left_sum(i):
        both = tree_sum(p_sums[i]).T
        p_own[mat if i else 1 - mat, :, 0:ROWS] = both[:RANK] + both[RANK:]

    y_beside = mat * 2 + 1 - y % 2
    y_across = (1 - mat) * 2 + 1 - y % 2
    top, low = pl.ds(0, HALF), pl.ds(HALF, HALF)

    def wait_load(i):
        for copy in loads[i]:
            copy.wait()

    right_load.wait()
    for i in range(4):
        wait_load(i)
        for yy in ((y_far, y_across), (y_beside, y))[i // 2]:
            combine(i, yy)
            left_product(i, yy)
        if i % 2 == 1:
            left_sum(i // 2)
    pl.semaphore_wait(barrier, len(z_peers) + len(near_peers))
    to_core("c_far", y_far)

    ranks = pl.ds(pl.multiple_of(c * 16, 16), 16)

    def to_place(k, cc):
        part = p_own.at[(y + k) % 4 // 2, pl.ds(pl.multiple_of(cc * 16, 16), 16)]
        send("p_y", part, p_y.at[2 * y + c], at(y_=(y + k) % 4, c_=cc))

    for k in (2, 1, 3):
        for cc in (c, 1 - c):
            to_place(k, cc)

    def ring_first(part):
        cols = RING[part]
        send("r_top%d" % part, s_buf.at[y_far, top, cols], r1.at[0, :, cols], y_at(1))
        send("r_low%d" % part, s_buf.at[y_far, low, cols], r1.at[1, :, cols], y_at(3))
        net.expect("r_top%d" % part, r1.at[0, :, cols], y_at(1))
        net.expect("r_low%d" % part, r1.at[1, :, cols], y_at(3))

    def ring_second(part):
        cols, tag = RING[part], "r_end%d" % part
        send(tag, s_buf.at[y_next, low, cols], r2.at[0, :, cols], y_at(1))
        send(tag, s_buf.at[y_prev, top, cols], r2.at[1, :, cols], y_at(3))
        take("r_top%d" % part)
        s_buf[y_next, top, cols] += r1[0, :, cols]
        send(tag, s_buf.at[y_next, top, cols], r2.at[2, :, cols], y_at(1))
        take("r_low%d" % part)
        s_buf[y_prev, low, cols] += r1[1, :, cols]
        send(tag, s_buf.at[y_prev, low, cols], r2.at[3, :, cols], y_at(3))
        net.expect(tag, r2.at[:, :, cols], core_peer)

    def ring_end(part):
        cols = RING[part]
        take("r_end%d" % part)
        s_buf[y, top, cols] = (s_buf[y, top, cols] + r2[1, :, cols]) + r2[2, :, cols]
        s_buf[y, low, cols] = (s_buf[y, low, cols] + r2[0, :, cols]) + r2[3, :, cols]

    sum_cores("c_far", y_far)
    ring_first(0)
    ring_first(1)
    to_place(0, 1 - c)
    net.expect("p_y", p_y.at[pl.ds(0, 7)], core_peer)
    p_y[2 * y + c] = p_own[mat, ranks]
    to_core("c_across", y_across)
    to_core("c_beside", y_beside)
    to_core("c_own", y)
    sum_cores("c_across", y_across)
    sum_cores("c_beside", y_beside)
    sum_cores("c_own", y)

    take("p_y")
    p_x[x] = tree_sum([p_y[i] for i in range(8)])
    for k in (2, 1, 3):
        send("p_x", p_x.at[x], p_x.at[x], x_at(k))
    net.expect("p_x", p_x.at[pl.ds(0, 3)], core_peer)
    ring_second(0)

    take("p_x")
    p_z[z] = tree_sum([p_x[i] for i in range(4)])
    for k in (4, 3, 5, 2, 6, 1, 7):
        send("p_z", p_z.at[z], p_z.at[z], z_at(k))
    net.expect("p_z", p_z.at[pl.ds(0, 7)], core_peer)
    ring_second(1)
    take("p_z")
    p_full[ranks] = tree_sum([p_z[i] for i in range(8)]) * (1.0 / REPLICAS)
    send("p_full", p_full.at[ranks], p_full.at[ranks], core_peer)
    net.expect("p_full", p_full.at[pl.ds(pl.multiple_of(16 - c * 16, 16), 16)], core_peer)
    ring_end(0)
    take("p_full")

    near = (zl + 2) // 3
    far = 1 - near
    owner = (zl == 0) | (zl == 2)

    def cols_of(piece):
        return pl.ds(*PIECES[piece])

    def to_owner(h, piece):
        cols = cols_of(piece)
        return net.copy("z_sum%d" % piece, q_part.at[h, :, cols], z_part.at[zl, :, cols], at(zl_=2 * h))

    def from_owner(h, k, piece):
        mine = q_all.at[c, y, h, :, cols_of(piece)]
        return net.copy("half%d%d" % (h, piece), mine, mine, zl_at(k))

    left = jnp.concatenate(split(p_full[:, :ROWS]), axis=0)
    for piece in range(len(PIECES)):
        cols = cols_of(piece)
        if piece == len(PIECES) - 1:
            ring_end(1)
        hi, lo = split(s_buf[y, :, cols])
        prod = dot(left, hi, ((1,), (0,))) + dot(left, lo, ((1,), (0,)))
        q_part[:, :, cols] = (prod[:RANK] + prod[RANK:]).reshape(2, 16, PIECES[piece][1])
        for h in range(2):
            pl.when(zl != 2 * h)(to_owner(h, piece).start)

    @net.at_end
    def _():
        def sent(ref):
            net.copy("", ref, ref, core_peer).wait_send()

        sent(q_part.at[0])

        @pl.when(owner)
        def _():
            for _ in range(3):
                sent(q_part.at[0])

        @pl.when(jnp.logical_not(owner))
        def _():
            sent(q_part.at[1])

    w_t[mat, :, 0:ROWS] = left_times_inverse(p_full[:, :ROWS]) * (1.0 / REPLICAS)
    send("w", w_t.at[mat], w_t.at[mat], y_at(2))
    net.expect("w", w_t.at[1 - mat], y_at(2))

    def to_other_core(yy, half):
        part = q_all.at[c, yy, half]
        send("core", part, part, core_peer)

    for half, name in ((near, "near"), (far, "far")):
        for piece in range(len(PIECES)):
            cols = cols_of(piece)
            landing = [net.landing("half%d%d" % (h, piece), q_all.at[c, y, h, :, cols], core_peer) for h in range(2)]

            def land(half=half, landing=landing):
                for h in range(2):
                    pl.when(half == h)(landing[h])

            if name == "far":
                land()
            else:

                @pl.when(owner)
                def _(piece=piece, cols=cols):
                    z_part[zl, :, cols] = q_part[near, :, cols]
                    net.landing("z_sum%d" % piece, z_part.at[pl.ds(0, 3), :, cols], core_peer)()
                    q_all[c, y, near, :, cols] = tree_sum([z_part[i, :, cols] for i in range(4)])
                    for h in range(2):

                        @pl.when(near == h)
                        def _():
                            for k in (1, 2, 3):
                                from_owner(h, k, piece).start()

                pl.when(jnp.logical_not(owner))(land)
            part = q_all.at[c, y, half, :, cols]
            for k in (2, 1, 3):
                send("%s%d" % (name, k), part, part, y_at(k))
        for k in (1, 2, 3):
            net.expect("%s%d" % (name, k), q_all.at[c, (y + 4 - k) % 4, half], core_peer)
        to_other_core(y, half)
    net.expect("core", q_all.at[1 - c], core_peer)

    def decode_own(yy):
        out = decode(w_out[yy // 2], q_all[c, yy].reshape(RANK, WIDTH))
        cols = pl.ds(pl.multiple_of(yy % 2 * WIDTH, 128), WIDTH)
        decoded[yy // 2, :, cols] = out
        carried[yy // 2, :, cols] = comb[c, yy] - out

    for half, name in ((near, "near"), (far, "far")):
        for k in (1, 3, 2):
            take("%s%d" % (name, k))
            to_other_core((y + 4 - k) % 4, half)
        if name == "near":
            take("w")
            for i in range(MATS):
                hi, lo = split(w_t[i, :, 0:ROWS].T)
                w_out[i] = jnp.concatenate([hi, lo, hi, lo], axis=1)
    for k in (0, 1, 3, 2):
        decode_own((y + 4 - k) % 4)
    net.finish(
        [
            c_recv,
            r1,
            r2,
            p_y.at[pl.ds(0, 7)],
            p_x.at[pl.ds(0, 3)],
            p_z.at[pl.ds(0, 7)],
            p_full.at[pl.ds(0, 16)],
            w_t.at[0],
            q_all.at[0, pl.ds(0, 3)],
            q_all.at[0],
        ],
        core_peer,
    )


def write_kernel(comb, q_all, w_ref, own_decoded, own_carried, decoded, carried, d_buf, c_buf, sem):
    c = lax.axis_index("dp") % 2
    copies = []

    def write(cc, mat, d_ref, c_ref):
        cols = pl.ds(pl.multiple_of(cc * 2 * WIDTH, 128), 2 * WIDTH)
        for ref, to in ((d_ref, decoded.at[mat, :, cols]), (c_ref, carried.at[0, mat, :, cols])):
            copies.append(pltpu.make_async_copy(ref, to, sem.at[0]))
            copies[-1].start()

    for mat in range(MATS):
        write(c, mat, own_decoded.at[mat], own_carried.at[mat])
    for mat in range(MATS):
        for i in range(2):
            cols = pl.ds(i * WIDTH, WIDTH)
            out = decode(w_ref[mat], q_all[1 - c, 2 * mat + i].reshape(RANK, WIDTH))
            d_buf[mat, :, cols] = out
            c_buf[mat, :, cols] = comb[1 - c, 2 * mat + i] - out
        write(1 - c, mat, d_buf.at[mat], c_buf.at[mat])
    for copy in copies:
        copy.wait()


def reduce_call(gradient, feedback, right_initial, name="reduce", collective_id=0):
    right_t = jnp.swapaxes(right_initial, 1, 2)
    vmem = pl.BlockSpec(memory_space=pltpu.VMEM)
    hbm = pl.BlockSpec(memory_space=pltpu.HBM)
    dma = pltpu.SemaphoreType.DMA
    return pl.pallas_call(
        reduce_kernel,
        name=name,
        out_shape=(
            jax.ShapeDtypeStruct((2, 4, ROWS, WIDTH), F32),
            jax.ShapeDtypeStruct((2, 4, 2, 16, WIDTH), F32),
            jax.ShapeDtypeStruct((MATS, ROWS, 128), BF16),
            jax.ShapeDtypeStruct((MATS, ROWS, 2 * WIDTH), F32),
            jax.ShapeDtypeStruct((MATS, ROWS, 2 * WIDTH), F32),
        ),
        in_specs=[hbm] * 3,
        out_specs=(vmem,) * 5,
        scratch_shapes=[
            pltpu.VMEM((4, ROWS, 2 * WIDTH), BF16),
            pltpu.VMEM((4, ROWS, 2 * WIDTH), F32),
            pltpu.VMEM((MATS, RANK, COLS), F32),
            pltpu.VMEM((4, ROWS, WIDTH), F32),
            pltpu.VMEM((4, ROWS, WIDTH), F32),
            pltpu.VMEM((2, HALF, WIDTH), F32),
            pltpu.VMEM((4, HALF, WIDTH), F32),
            pltpu.VMEM((MATS, RANK, 128), F32),
            pltpu.VMEM((8, 16, 128), F32),
            pltpu.VMEM((4, 16, 128), F32),
            pltpu.VMEM((8, 16, 128), F32),
            pltpu.VMEM((RANK, 128), F32),
            pltpu.VMEM((MATS, RANK, 128), F32),
            pltpu.VMEM((2, 16, WIDTH), F32),
            pltpu.VMEM((4, 16, WIDTH), F32),
            dma((5,)),
            dma((1,)),
            dma((TAGS,)),
        ],
        compiler_params=pltpu.CompilerParams(
            collective_id=collective_id, has_side_effects=True, vmem_limit_bytes=VMEM_BYTES
        ),
    )(*(pltpu.with_memory_space_constraint(a, pltpu.HBM) for a in (gradient, feedback, right_t)))


def per_device(gradient, feedback, right_initial):
    vmem = pl.BlockSpec(memory_space=pltpu.VMEM)
    hbm = pl.BlockSpec(memory_space=pltpu.HBM)
    return pl.pallas_call(
        write_kernel,
        name="write",
        out_shape=(
            jax.ShapeDtypeStruct((MATS, ROWS, COLS), F32),
            jax.ShapeDtypeStruct((1, MATS, ROWS, COLS), F32),
        ),
        in_specs=[vmem] * 5,
        out_specs=(hbm, hbm),
        scratch_shapes=[
            pltpu.VMEM((MATS, ROWS, 2 * WIDTH), F32),
            pltpu.VMEM((MATS, ROWS, 2 * WIDTH), F32),
            pltpu.SemaphoreType.DMA((1,)),
        ],
        compiler_params=pltpu.CompilerParams(vmem_limit_bytes=VMEM_BYTES),
    )(*reduce_call(gradient, feedback, right_initial))


def solution(mesh):
    placed = (P("dp", None, None, "mp"), P("dp", None, None, "mp"), P(None, "mp", None))
    return jax.shard_map(
        per_device,
        mesh=mesh,
        in_specs=placed,
        out_specs=(P(None, None, "mp"), P("dp", None, None, "mp")),
        check_vma=False,
    )
```

```python
import jax
import jax.numpy as jnp
from jax import lax
from jax.experimental import pallas as pl
from jax.experimental.pallas import tpu as pltpu
from jax.sharding import PartitionSpec as P

MESH = pl.DeviceIdType.MESH
F32 = jnp.float32
BF16 = jnp.bfloat16
MATS, ROWS, RANK, COLS = 2, 96, 32, 3584
WIDTH = 896
PIECES = ((0, 384), (384, 256), (640, 256))
RING = (pl.ds(0, 640), pl.ds(640, 256))
HALF = ROWS // 2
REPLICAS = 32
BLOCK = 4
TAGS = 28
VMEM_BYTES = 32 << 20


def split(a):
    hi = a.astype(BF16)
    return hi, (a - hi.astype(F32)).astype(BF16)


def dot(a, b, contract):
    return lax.dot_general(a, b, ((contract[0], contract[1]), ((), ())), preferred_element_type=F32)


def exact(a, b, contract):
    return lax.dot_general(
        a, b, ((contract[0], contract[1]), ((), ())), precision=lax.Precision.HIGHEST, preferred_element_type=F32
    )


def left_times_inverse(p_t):
    gram = exact(p_t, p_t, ((1,), (1,)))
    row = lax.broadcasted_iota(jnp.int32, (RANK, RANK), 0)
    col = lax.broadcasted_iota(jnp.int32, (RANK, RANK), 1)
    eye = jnp.where(row == col, 1.0, 0.0).astype(F32)
    inv = eye
    for start in range(0, RANK, BLOCK):
        columns = [jnp.broadcast_to(gram[:, k : k + 1], (RANK, RANK)) for k in range(start, start + BLOCK)]
        for j, k in enumerate(range(start, start + BLOCK)):
            factor = jnp.where(row > k, columns[j] * (1.0 / columns[j][k : k + 1, :]), 0.0)
            gram, inv = (a - factor * a[k : k + 1, :] for a in (gram, inv))
            columns[j + 1 :] = [a - factor * a[k : k + 1, :] for a in columns[j + 1 :]]
    diag = jnp.sum(gram * eye, axis=1, keepdims=True)
    l_inv = inv * lax.rsqrt(diag)
    orth_t = exact(l_inv, p_t, ((1,), (0,)))
    return exact(l_inv, orth_t, ((0,), (0,)))


def decode(left, q):
    hi, lo = split(q)
    return dot(left, jnp.concatenate([hi, hi, lo, lo], axis=0), ((1,), (0,)))


class Net:
    def __init__(self, send_sem, recv_sem):
        self.send_sem, self.recv_sem = send_sem, recv_sem
        self.tags, self.due, self.last = {"": 0}, {}, []

    def copy(self, tag, src, dst, to):
        return pltpu.make_async_remote_copy(
            src_ref=src,
            dst_ref=dst,
            send_sem=self.send_sem.at[0],
            recv_sem=self.recv_sem.at[self.tags.setdefault(tag, len(self.tags))],
            device_id=to,
            device_id_type=MESH,
        )

    def send(self, tag, src, dst, to):
        self.copy(tag, src, dst, to).start()

    def landing(self, tag, ref, to):
        return self.copy(tag, ref, ref, to).wait_recv

    def expect(self, tag, ref, to):
        self.due[tag] = self.landing(tag, ref, to)

    def take(self, tag):
        self.due.pop(tag)()

    def at_end(self, step):
        self.last.append(step)

    def finish(self, totals, to):
        for tag in list(self.due):
            self.take(tag)
        for ref in totals:
            self.copy("", ref, ref, to).wait_send()
        for step in self.last:
            step()


def tree_sum(terms):
    while len(terms) > 1:
        terms = [a + b for a, b in zip(terms[::2], terms[1::2])]
    return terms[0]


def reduce_kernel(
    g_hbm, f_hbm, r_hbm, comb, q_all, w_out, decoded, carried,
    g_buf, f_buf, r_buf, c_recv, s_buf, r1, r2, p_own, p_y, p_x, p_z, p_full, w_t, q_part, z_part,
    load_sem, send_sem, recv_sem,
):
    d = lax.axis_index("dp")
    m = lax.axis_index("mp")
    zl, y, c = d // 8, (d // 2) % 4, d % 2
    x, zh = m // 2, m % 2
    z = zh * 4 + zl
    net = Net(send_sem, recv_sem)
    send, take = net.send, net.take

    def at(zl_=zl, y_=y, c_=c, x_=x, zh_=zh):
        return (zl_ * 8 + y_ * 2 + c_, x_ * 2 + zh_)

    def y_at(k):
        return at(y_=(y + k) % 4)

    def x_at(k):
        return at(x_=(x + k) % 4)

    def z_at(k):
        to = (z + k) % 8
        return at(zl_=to % 4, zh_=to // 4)

    def zl_at(k):
        return at(zl_=(zl + k) % 4)

    core_peer = at(c_=1 - c)
    y_next, y_prev, y_far = (y + 1) % 4, (y + 3) % 4, (y + 2) % 4
    mat = y // 2

    barrier = pltpu.get_barrier_semaphore()

    def greet(peers):
        for to in peers:
            pl.semaphore_signal(barrier, inc=1, device_id=to, device_id_type=MESH)

    z_peers = [z_at(k) for k in (4, 3, 5, 2, 6, 1, 7)]
    greet(z_peers)

    pairs = [(1 - c, 1 - mat), (c, 1 - mat), (1 - c, mat), (c, mat)]
    loads = []
    for i, (cc, mm) in enumerate(pairs):
        cols = pl.ds(pl.multiple_of(cc * 2 * WIDTH, 128), 2 * WIDTH)
        loads.append(
            (
                pltpu.make_async_copy(f_hbm.at[0, mm, :, cols], f_buf.at[i], load_sem.at[i]),
                pltpu.make_async_copy(g_hbm.at[0, mm, :, cols], g_buf.at[i], load_sem.at[i]),
            )
        )
    right_load = pltpu.make_async_copy(r_hbm, r_buf, load_sem.at[4])
    right_load.start()
    for copies in loads:
        for copy in copies:
            copy.start()

    near_peers = [core_peer] + [at(y_=(y + k) % 4, c_=cc) for k in (2, 1, 3) for cc in (c, 1 - c)]
    near_peers += [x_at(k) for k in (2, 1, 3)]
    greet(near_peers)
    p_own[...] = jnp.zeros(p_own.shape, F32)
    p_sums = {}

    def combine(i, yy):
        cc = pairs[i][0]
        cols = pl.ds(pl.multiple_of(yy % 2 * WIDTH, 128), WIDTH)
        comb[cc, yy] = g_buf[i, :, cols].astype(F32) + f_buf[i, :, cols]

    def to_core(name, yy):
        send(name, comb.at[1 - c, yy], c_recv.at[yy], core_peer)
        net.expect(name, c_recv.at[yy], core_peer)

    def sum_cores(name, yy):
        take(name)
        s_buf[yy] = comb[c, yy] + c_recv[yy]

    def left_product(i, yy):
        hi, lo = split(comb[pairs[i][0], yy])
        cols = pl.ds(pl.multiple_of((2 * pairs[i][0] + yy % 2) * WIDTH, 128), WIDTH)
        right = jnp.concatenate(split(r_buf[yy // 2, :, cols]), axis=0)
        both = dot(jnp.concatenate([hi, lo], axis=0), right, ((1,), (1,)))
        p_sums.setdefault(i // 2, []).append(both[:ROWS] + both[ROWS:])

    def left_sum(i):
        both = tree_sum(p_sums[i]).T
        p_own[mat if i else 1 - mat, :, 0:ROWS] = both[:RANK] + both[RANK:]

    y_beside = mat * 2 + 1 - y % 2
    y_across = (1 - mat) * 2 + 1 - y % 2
    top, low = pl.ds(0, HALF), pl.ds(HALF, HALF)

    def wait_load(i):
        for copy in loads[i]:
            copy.wait()

    right_load.wait()
    for i in range(4):
        wait_load(i)
        for yy in ((y_far, y_across), (y_beside, y))[i // 2]:
            combine(i, yy)
            left_product(i, yy)
        if i % 2 == 1:
            left_sum(i // 2)
    pl.semaphore_wait(barrier, len(z_peers) + len(near_peers))

    ranks = pl.ds(pl.multiple_of(c * 16, 16), 16)

    def to_place(k, cc):
        part = p_own.at[(y + k) % 4 // 2, pl.ds(pl.multiple_of(cc * 16, 16), 16)]
        send("p_y", part, p_y.at[2 * y + c], at(y_=(y + k) % 4, c_=cc))

    for k in (2, 1, 3):
        for cc in (c, 1 - c):
            to_place(k, cc)
        if k == 2:
            to_core("c_far", y_far)
    to_place(0, 1 - c)
    net.expect("p_y", p_y.at[pl.ds(0, 7)], core_peer)
    p_y[2 * y + c] = p_own[mat, ranks]
    to_core("c_across", y_across)
    to_core("c_beside", y_beside)
    to_core("c_own", y)

    def ring_first(part):
        cols = RING[part]
        send("r_far%d" % part, s_buf.at[y_far, top, cols], r1.at[0, :, cols], y_at(1))
        send("r_far%d" % part, s_buf.at[y_far, low, cols], r1.at[1, :, cols], y_at(3))
        net.expect("r_far%d" % part, r1.at[:, :, cols], core_peer)

    def ring_ready(part):
        cols, tag = RING[part], "r_end%d" % part
        send(tag, s_buf.at[y_next, low, cols], r2.at[0, :, cols], y_at(1))
        send(tag, s_buf.at[y_prev, top, cols], r2.at[1, :, cols], y_at(3))

    def ring_second(part):
        cols, tag = RING[part], "r_end%d" % part
        take("r_far%d" % part)
        s_buf[y_next, top, cols] += r1[0, :, cols]
        send(tag, s_buf.at[y_next, top, cols], r2.at[2, :, cols], y_at(1))
        s_buf[y_prev, low, cols] += r1[1, :, cols]
        send(tag, s_buf.at[y_prev, low, cols], r2.at[3, :, cols], y_at(3))
        net.expect(tag, r2.at[:, :, cols], core_peer)

    def ring_end(part):
        cols = RING[part]
        take("r_end%d" % part)
        s_buf[y, top, cols] = (s_buf[y, top, cols] + r2[1, :, cols]) + r2[2, :, cols]
        s_buf[y, low, cols] = (s_buf[y, low, cols] + r2[0, :, cols]) + r2[3, :, cols]

    sum_cores("c_far", y_far)
    ring_first(0)
    ring_first(1)

    take("p_y")
    p_x[x] = tree_sum([p_y[i] for i in range(8)])
    for k in (2, 1, 3):
        send("p_x", p_x.at[x], p_x.at[x], x_at(k))
    net.expect("p_x", p_x.at[pl.ds(0, 3)], core_peer)
    sum_cores("c_across", y_across)
    sum_cores("c_beside", y_beside)
    ring_ready(0)

    take("p_x")
    p_z[z] = tree_sum([p_x[i] for i in range(4)])
    for k in (4, 3, 5, 2, 6, 1, 7):
        send("p_z", p_z.at[z], p_z.at[z], z_at(k))
    net.expect("p_z", p_z.at[pl.ds(0, 7)], core_peer)
    ring_second(0)
    ring_ready(1)
    ring_second(1)
    sum_cores("c_own", y)
    take("p_z")
    p_full[ranks] = tree_sum([p_z[i] for i in range(8)]) * (1.0 / REPLICAS)
    send("p_full", p_full.at[ranks], p_full.at[ranks], core_peer)
    net.expect("p_full", p_full.at[pl.ds(pl.multiple_of(16 - c * 16, 16), 16)], core_peer)
    ring_end(0)
    halves = [split(s_buf[y, :, pl.ds(*PIECES[piece])]) for piece in range(len(PIECES) - 1)]
    take("p_full")

    near = (zl + 2) // 3
    far = 1 - near
    owner = (zl == 0) | (zl == 2)

    def cols_of(piece):
        return pl.ds(*PIECES[piece])

    def to_owner(h, piece):
        cols = cols_of(piece)
        return net.copy("z_sum%d" % piece, q_part.at[h, :, cols], z_part.at[zl, :, cols], at(zl_=2 * h))

    def from_owner(h, k, piece):
        mine = q_all.at[c, y, h, :, cols_of(piece)]
        return net.copy("half%d%d" % (h, piece), mine, mine, zl_at(k))

    left = jnp.concatenate(split(p_full[:, :ROWS]), axis=0)
    for piece in range(len(PIECES)):
        cols = cols_of(piece)
        if piece == len(PIECES) - 1:
            ring_end(1)
            halves.append(split(s_buf[y, :, cols]))
        hi, lo = halves[piece]
        prod = dot(left, hi, ((1,), (0,))) + dot(left, lo, ((1,), (0,)))
        q_part[:, :, cols] = (prod[:RANK] + prod[RANK:]).reshape(2, 16, PIECES[piece][1])
        for h in range(2):
            pl.when(zl != 2 * h)(to_owner(h, piece).start)

    @net.at_end
    def _():
        def sent(ref):
            net.copy("", ref, ref, core_peer).wait_send()

        sent(q_part.at[0])

        @pl.when(owner)
        def _():
            for _ in range(3):
                sent(q_part.at[0])

        @pl.when(jnp.logical_not(owner))
        def _():
            sent(q_part.at[1])

    w_t[mat, :, 0:ROWS] = left_times_inverse(p_full[:, :ROWS]) * (1.0 / REPLICAS)
    send("w", w_t.at[mat], w_t.at[mat], y_at(2))
    net.expect("w", w_t.at[1 - mat], y_at(2))

    def to_other_core(yy, half):
        part = q_all.at[c, yy, half]
        send("core", part, part, core_peer)

    for half, name in ((near, "near"), (far, "far")):
        for piece in range(len(PIECES)):
            cols = cols_of(piece)
            landing = [net.landing("half%d%d" % (h, piece), q_all.at[c, y, h, :, cols], core_peer) for h in range(2)]

            def land(half=half, landing=landing):
                for h in range(2):
                    pl.when(half == h)(landing[h])

            if name == "far":
                land()
            else:

                @pl.when(owner)
                def _(piece=piece, cols=cols):
                    z_part[zl, :, cols] = q_part[near, :, cols]
                    net.landing("z_sum%d" % piece, z_part.at[pl.ds(0, 3), :, cols], core_peer)()
                    q_all[c, y, near, :, cols] = tree_sum([z_part[i, :, cols] for i in range(4)])

                @pl.when(zl == 2)
                def _(piece=piece):
                    for k in (2, 3, 1):
                        from_owner(1, k, piece).start()

                pl.when(jnp.logical_not(owner))(land)
            part = q_all.at[c, y, half, :, cols]
            for k in (2, 1, 3):
                send("far%d" % k if name == "far" else "near", part, part, y_at(k))
            if name == "near":

                @pl.when(zl == 0)
                def _(piece=piece):
                    for k in (1, 2, 3):
                        from_owner(0, k, piece).start()

        if name == "near":
            net.expect("near", q_all.at[c, pl.ds(0, 3), half], core_peer)
        else:
            for k in (1, 2, 3):
                net.expect("far%d" % k, q_all.at[c, (y + 4 - k) % 4, half], core_peer)
        to_other_core(y, half)
    net.expect("core", q_all.at[1 - c], core_peer)

    def decode_own(yy):
        out = decode(w_out[yy // 2], q_all[c, yy].reshape(RANK, WIDTH))
        cols = pl.ds(pl.multiple_of(yy % 2 * WIDTH, 128), WIDTH)
        decoded[yy // 2, :, cols] = out
        carried[yy // 2, :, cols] = comb[c, yy] - out

    for half, name in ((near, "near"), (far, "far")):
        if name == "near":
            take("near")
        for k in (1, 3, 2):
            if name == "far":
                take("far%d" % k)
            to_other_core((y + 4 - k) % 4, half)
        if name == "near":
            take("w")
            for i in range(MATS):
                hi, lo = split(w_t[i, :, 0:ROWS].T)
                w_out[i] = jnp.concatenate([hi, lo, hi, lo], axis=1)
    for k in (0, 1, 3, 2):
        decode_own((y + 4 - k) % 4)
    net.finish(
        [
            c_recv,
            r1,
            r2,
            p_y.at[pl.ds(0, 7)],
            p_x.at[pl.ds(0, 3)],
            p_z.at[pl.ds(0, 7)],
            p_full.at[pl.ds(0, 16)],
            w_t.at[0],
            q_all.at[0, pl.ds(0, 3)],
            q_all.at[0],
        ],
        core_peer,
    )


def write_kernel(comb, q_all, w_ref, own_decoded, own_carried, decoded, carried, d_buf, c_buf, sem):
    c = lax.axis_index("dp") % 2
    copies = []

    def write(cc, mat, d_ref, c_ref):
        cols = pl.ds(pl.multiple_of(cc * 2 * WIDTH, 128), 2 * WIDTH)
        for ref, to in ((d_ref, decoded.at[mat, :, cols]), (c_ref, carried.at[0, mat, :, cols])):
            copies.append(pltpu.make_async_copy(ref, to, sem.at[0]))
            copies[-1].start()

    for mat in range(MATS):
        write(c, mat, own_decoded.at[mat], own_carried.at[mat])
    for mat in range(MATS):
        for i in range(2):
            cols = pl.ds(i * WIDTH, WIDTH)
            out = decode(w_ref[mat], q_all[1 - c, 2 * mat + i].reshape(RANK, WIDTH))
            d_buf[mat, :, cols] = out
            c_buf[mat, :, cols] = comb[1 - c, 2 * mat + i] - out
        write(1 - c, mat, d_buf.at[mat], c_buf.at[mat])
    for copy in copies:
        copy.wait()


def reduce_call(gradient, feedback, right_initial, name="reduce", collective_id=0):
    right_t = jnp.swapaxes(right_initial, 1, 2)
    vmem = pl.BlockSpec(memory_space=pltpu.VMEM)
    hbm = pl.BlockSpec(memory_space=pltpu.HBM)
    dma = pltpu.SemaphoreType.DMA
    return pl.pallas_call(
        reduce_kernel,
        name=name,
        out_shape=(
            jax.ShapeDtypeStruct((2, 4, ROWS, WIDTH), F32),
            jax.ShapeDtypeStruct((2, 4, 2, 16, WIDTH), F32),
            jax.ShapeDtypeStruct((MATS, ROWS, 128), BF16),
            jax.ShapeDtypeStruct((MATS, ROWS, 2 * WIDTH), F32),
            jax.ShapeDtypeStruct((MATS, ROWS, 2 * WIDTH), F32),
        ),
        in_specs=[hbm] * 3,
        out_specs=(vmem,) * 5,
        scratch_shapes=[
            pltpu.VMEM((4, ROWS, 2 * WIDTH), BF16),
            pltpu.VMEM((4, ROWS, 2 * WIDTH), F32),
            pltpu.VMEM((MATS, RANK, COLS), F32),
            pltpu.VMEM((4, ROWS, WIDTH), F32),
            pltpu.VMEM((4, ROWS, WIDTH), F32),
            pltpu.VMEM((2, HALF, WIDTH), F32),
            pltpu.VMEM((4, HALF, WIDTH), F32),
            pltpu.VMEM((MATS, RANK, 128), F32),
            pltpu.VMEM((8, 16, 128), F32),
            pltpu.VMEM((4, 16, 128), F32),
            pltpu.VMEM((8, 16, 128), F32),
            pltpu.VMEM((RANK, 128), F32),
            pltpu.VMEM((MATS, RANK, 128), F32),
            pltpu.VMEM((2, 16, WIDTH), F32),
            pltpu.VMEM((4, 16, WIDTH), F32),
            dma((5,)),
            dma((1,)),
            dma((TAGS,)),
        ],
        compiler_params=pltpu.CompilerParams(
            collective_id=collective_id, has_side_effects=True, vmem_limit_bytes=VMEM_BYTES
        ),
    )(*(pltpu.with_memory_space_constraint(a, pltpu.HBM) for a in (gradient, feedback, right_t)))


def per_device(gradient, feedback, right_initial):
    vmem = pl.BlockSpec(memory_space=pltpu.VMEM)
    hbm = pl.BlockSpec(memory_space=pltpu.HBM)
    return pl.pallas_call(
        write_kernel,
        name="write",
        out_shape=(
            jax.ShapeDtypeStruct((MATS, ROWS, COLS), F32),
            jax.ShapeDtypeStruct((1, MATS, ROWS, COLS), F32),
        ),
        in_specs=[vmem] * 5,
        out_specs=(hbm, hbm),
        scratch_shapes=[
            pltpu.VMEM((MATS, ROWS, 2 * WIDTH), F32),
            pltpu.VMEM((MATS, ROWS, 2 * WIDTH), F32),
            pltpu.SemaphoreType.DMA((1,)),
        ],
        compiler_params=pltpu.CompilerParams(vmem_limit_bytes=VMEM_BYTES),
    )(*reduce_call(gradient, feedback, right_initial))


def solution(mesh):
    placed = (P("dp", None, None, "mp"), P("dp", None, None, "mp"), P(None, "mp", None))
    return jax.shard_map(
        per_device,
        mesh=mesh,
        in_specs=placed,
        out_specs=(P(None, None, "mp"), P("dp", None, None, "mp")),
        check_vma=False,
    )
```

```python
import jax
import jax.numpy as jnp
from jax import lax
from jax.experimental import pallas as pl
from jax.experimental.pallas import tpu as pltpu
from jax.sharding import PartitionSpec as P

MESH = pl.DeviceIdType.MESH
F32 = jnp.float32
BF16 = jnp.bfloat16
MATS, ROWS, RANK, COLS = 2, 96, 32, 3584
WIDTH = 896
PIECES = ((0, 384), (384, 256), (640, 256))
RING = (pl.ds(0, 640), pl.ds(640, 256))
HALF = ROWS // 2
REPLICAS = 32
BLOCK = 4
TAGS = 28
VMEM_BYTES = 32 << 20


def split(a):
    hi = a.astype(BF16)
    return hi, (a - hi.astype(F32)).astype(BF16)


def dot(a, b, contract):
    return lax.dot_general(a, b, ((contract[0], contract[1]), ((), ())), preferred_element_type=F32)


def exact(a, b, contract):
    return lax.dot_general(
        a, b, ((contract[0], contract[1]), ((), ())), precision=lax.Precision.HIGHEST, preferred_element_type=F32
    )


def left_times_inverse(p_t):
    gram = exact(p_t, p_t, ((1,), (1,)))
    row = lax.broadcasted_iota(jnp.int32, (RANK, RANK), 0)
    col = lax.broadcasted_iota(jnp.int32, (RANK, RANK), 1)
    eye = jnp.where(row == col, 1.0, 0.0).astype(F32)
    inv = eye
    for start in range(0, RANK, BLOCK):
        columns = [jnp.broadcast_to(gram[:, k : k + 1], (RANK, RANK)) for k in range(start, start + BLOCK)]
        for j, k in enumerate(range(start, start + BLOCK)):
            factor = jnp.where(row > k, columns[j] * (1.0 / columns[j][k : k + 1, :]), 0.0)
            gram, inv = (a - factor * a[k : k + 1, :] for a in (gram, inv))
            columns[j + 1 :] = [a - factor * a[k : k + 1, :] for a in columns[j + 1 :]]
    diag = jnp.sum(gram * eye, axis=1, keepdims=True)
    l_inv = inv * lax.rsqrt(diag)
    orth_t = exact(l_inv, p_t, ((1,), (0,)))
    return exact(l_inv, orth_t, ((0,), (0,)))


def decode(left, q):
    hi, lo = split(q)
    return dot(left, jnp.concatenate([hi, hi, lo, lo], axis=0), ((1,), (0,)))


class Net:
    def __init__(self, send_sem, recv_sem):
        self.send_sem, self.recv_sem = send_sem, recv_sem
        self.tags, self.due, self.last = {"": 0}, {}, []

    def copy(self, tag, src, dst, to):
        return pltpu.make_async_remote_copy(
            src_ref=src,
            dst_ref=dst,
            send_sem=self.send_sem.at[0],
            recv_sem=self.recv_sem.at[self.tags.setdefault(tag, len(self.tags))],
            device_id=to,
            device_id_type=MESH,
        )

    def send(self, tag, src, dst, to):
        self.copy(tag, src, dst, to).start()

    def landing(self, tag, ref, to):
        return self.copy(tag, ref, ref, to).wait_recv

    def expect(self, tag, ref, to):
        self.due[tag] = self.landing(tag, ref, to)

    def take(self, tag):
        self.due.pop(tag)()

    def at_end(self, step):
        self.last.append(step)

    def finish(self, totals, to):
        for tag in list(self.due):
            self.take(tag)
        for ref in totals:
            self.copy("", ref, ref, to).wait_send()
        for step in self.last:
            step()


def tree_sum(terms):
    while len(terms) > 1:
        terms = [a + b for a, b in zip(terms[::2], terms[1::2])]
    return terms[0]


def reduce_kernel(
    g_hbm, f_hbm, r_hbm, comb, q_all, w_out, decoded, carried,
    g_buf, f_buf, r_buf, c_recv, s_buf, r1, r2, p_own, p_y, p_x, p_z, p_full, w_t, q_part, z_part,
    load_sem, send_sem, recv_sem,
):
    d = lax.axis_index("dp")
    m = lax.axis_index("mp")
    zl, y, c = d // 8, (d // 2) % 4, d % 2
    x, zh = m // 2, m % 2
    z = zh * 4 + zl
    net = Net(send_sem, recv_sem)
    send, take = net.send, net.take

    def at(zl_=zl, y_=y, c_=c, x_=x, zh_=zh):
        return (zl_ * 8 + y_ * 2 + c_, x_ * 2 + zh_)

    def y_at(k):
        return at(y_=(y + k) % 4)

    def x_at(k):
        return at(x_=(x + k) % 4)

    def z_at(k):
        to = (z + k) % 8
        return at(zl_=to % 4, zh_=to // 4)

    def zl_at(k):
        return at(zl_=(zl + k) % 4)

    core_peer = at(c_=1 - c)
    y_next, y_prev, y_far = (y + 1) % 4, (y + 3) % 4, (y + 2) % 4
    mat = y // 2

    barrier = pltpu.get_barrier_semaphore()

    def greet(peers):
        for to in peers:
            pl.semaphore_signal(barrier, inc=1, device_id=to, device_id_type=MESH)

    z_peers = [z_at(k) for k in (4, 3, 5, 2, 6, 1, 7)]
    greet(z_peers)

    pairs = [(1 - c, 1 - mat), (c, 1 - mat), (1 - c, mat), (c, mat)]
    loads = []
    for i, (cc, mm) in enumerate(pairs):
        cols = pl.ds(pl.multiple_of(cc * 2 * WIDTH, 128), 2 * WIDTH)
        loads.append(
            (
                pltpu.make_async_copy(f_hbm.at[0, mm, :, cols], f_buf.at[i], load_sem.at[i]),
                pltpu.make_async_copy(g_hbm.at[0, mm, :, cols], g_buf.at[i], load_sem.at[i]),
            )
        )
    right_load = pltpu.make_async_copy(r_hbm, r_buf, load_sem.at[4])
    right_load.start()
    for copies in loads:
        for copy in copies:
            copy.start()

    near_peers = [core_peer] + [at(y_=(y + k) % 4, c_=cc) for k in (2, 1, 3) for cc in (c, 1 - c)]
    near_peers += [x_at(k) for k in (2, 1, 3)]
    greet(near_peers)
    p_own[...] = jnp.zeros(p_own.shape, F32)
    p_sums = {}

    def combine(i, yy):
        cc = pairs[i][0]
        cols = pl.ds(pl.multiple_of(yy % 2 * WIDTH, 128), WIDTH)
        comb[cc, yy] = g_buf[i, :, cols].astype(F32) + f_buf[i, :, cols]

    def to_core(name, yy):
        send(name, comb.at[1 - c, yy], c_recv.at[yy], core_peer)
        net.expect(name, c_recv.at[yy], core_peer)

    def sum_cores(name, yy):
        take(name)
        s_buf[yy] = comb[c, yy] + c_recv[yy]

    def left_product(i, yy):
        hi, lo = split(comb[pairs[i][0], yy])
        cols = pl.ds(pl.multiple_of((2 * pairs[i][0] + yy % 2) * WIDTH, 128), WIDTH)
        right = jnp.concatenate(split(r_buf[yy // 2, :, cols]), axis=0)
        both = dot(jnp.concatenate([hi, lo], axis=0), right, ((1,), (1,)))
        p_sums.setdefault(i // 2, []).append(both[:ROWS] + both[ROWS:])

    def left_sum(i):
        both = tree_sum(p_sums[i]).T
        p_own[mat if i else 1 - mat, :, 0:ROWS] = both[:RANK] + both[RANK:]

    y_beside = mat * 2 + 1 - y % 2
    y_across = (1 - mat) * 2 + 1 - y % 2
    top, low = pl.ds(0, HALF), pl.ds(HALF, HALF)

    def wait_load(i):
        for copy in loads[i]:
            copy.wait()

    ranks = pl.ds(pl.multiple_of(c * 16, 16), 16)
    k_other, k_same = 3 - 2 * (y % 2), 1 + 2 * (y % 2)

    def to_place(k, cc):
        part = p_own.at[(y + k) % 4 // 2, pl.ds(pl.multiple_of(cc * 16, 16), 16)]
        send("p_y", part, p_y.at[2 * y + c], at(y_=(y + k) % 4, c_=cc))

    def other_matrix():
        pl.semaphore_wait(barrier, len(z_peers) + len(near_peers))
        for k in (2, k_other):
            for cc in (c, 1 - c):
                to_place(k, cc)

    right_load.wait()
    for i in range(4):
        wait_load(i)
        for yy in ((y_far, y_across), (y_beside, y))[i // 2]:
            combine(i, yy)
            left_product(i, yy)
        if i % 2 == 1:
            left_sum(i // 2)
            pl.when(z >= 4 if i == 1 else z < 4)(other_matrix)
    to_core("c_far", y_far)
    for cc in (c, 1 - c):
        to_place(k_same, cc)
    to_place(0, 1 - c)
    net.expect("p_y", p_y.at[pl.ds(0, 7)], core_peer)
    p_y[2 * y + c] = p_own[mat, ranks]
    to_core("c_across", y_across)
    to_core("c_beside", y_beside)
    to_core("c_own", y)

    def ring_first(part):
        cols = RING[part]
        send("r_far%d" % part, s_buf.at[y_far, top, cols], r1.at[0, :, cols], y_at(1))
        send("r_far%d" % part, s_buf.at[y_far, low, cols], r1.at[1, :, cols], y_at(3))
        net.expect("r_far%d" % part, r1.at[:, :, cols], core_peer)

    def ring_ready(part):
        cols, tag = RING[part], "r_end%d" % part
        send(tag, s_buf.at[y_next, low, cols], r2.at[0, :, cols], y_at(1))
        send(tag, s_buf.at[y_prev, top, cols], r2.at[1, :, cols], y_at(3))

    def ring_second(part):
        cols, tag = RING[part], "r_end%d" % part
        take("r_far%d" % part)
        s_buf[y_next, top, cols] += r1[0, :, cols]
        send(tag, s_buf.at[y_next, top, cols], r2.at[2, :, cols], y_at(1))
        s_buf[y_prev, low, cols] += r1[1, :, cols]
        send(tag, s_buf.at[y_prev, low, cols], r2.at[3, :, cols], y_at(3))
        net.expect(tag, r2.at[:, :, cols], core_peer)

    def ring_end(part):
        cols = RING[part]
        take("r_end%d" % part)
        s_buf[y, top, cols] = (s_buf[y, top, cols] + r2[1, :, cols]) + r2[2, :, cols]
        s_buf[y, low, cols] = (s_buf[y, low, cols] + r2[0, :, cols]) + r2[3, :, cols]

    sum_cores("c_far", y_far)
    ring_first(0)
    ring_first(1)

    take("p_y")
    p_x[x] = tree_sum([p_y[i] for i in range(8)])
    for k in (2, 1, 3):
        send("p_x", p_x.at[x], p_x.at[x], x_at(k))
    net.expect("p_x", p_x.at[pl.ds(0, 3)], core_peer)
    sum_cores("c_across", y_across)
    sum_cores("c_beside", y_beside)
    ring_ready(0)

    take("p_x")
    p_z[z] = tree_sum([p_x[i] for i in range(4)])
    for k in (4, 3, 5, 2, 6, 1, 7):
        send("p_z", p_z.at[z], p_z.at[z], z_at(k))
    net.expect("p_z", p_z.at[pl.ds(0, 7)], core_peer)
    ring_second(0)
    ring_ready(1)
    ring_second(1)
    sum_cores("c_own", y)
    take("p_z")
    p_full[ranks] = tree_sum([p_z[i] for i in range(8)]) * (1.0 / REPLICAS)
    send("p_full", p_full.at[ranks], p_full.at[ranks], core_peer)
    net.expect("p_full", p_full.at[pl.ds(pl.multiple_of(16 - c * 16, 16), 16)], core_peer)
    ring_end(0)
    halves = [split(s_buf[y, :, pl.ds(*PIECES[piece])]) for piece in range(len(PIECES) - 1)]
    take("p_full")

    near = (zl + 2) // 3
    far = 1 - near
    owner = (zl == 0) | (zl == 2)

    def cols_of(piece):
        return pl.ds(*PIECES[piece])

    def to_owner(h, piece):
        cols = cols_of(piece)
        return net.copy("z_sum%d" % piece, q_part.at[h, :, cols], z_part.at[zl, :, cols], at(zl_=2 * h))

    def from_owner(h, k, piece):
        mine = q_all.at[c, y, h, :, cols_of(piece)]
        return net.copy("half%d%d" % (h, piece), mine, mine, zl_at(k))

    left = jnp.concatenate(split(p_full[:, :ROWS]), axis=0)
    for piece in range(len(PIECES)):
        cols = cols_of(piece)
        if piece == len(PIECES) - 1:
            ring_end(1)
            halves.append(split(s_buf[y, :, cols]))
        hi, lo = halves[piece]
        prod = dot(left, hi, ((1,), (0,))) + dot(left, lo, ((1,), (0,)))
        q_part[:, :, cols] = (prod[:RANK] + prod[RANK:]).reshape(2, 16, PIECES[piece][1])
        for h in range(2):
            pl.when(zl != 2 * h)(to_owner(h, piece).start)

    @net.at_end
    def _():
        def sent(ref):
            net.copy("", ref, ref, core_peer).wait_send()

        sent(q_part.at[0])

        @pl.when(owner)
        def _():
            for _ in range(3):
                sent(q_part.at[0])

        @pl.when(jnp.logical_not(owner))
        def _():
            sent(q_part.at[1])

    w_t[mat, :, 0:ROWS] = left_times_inverse(p_full[:, :ROWS]) * (1.0 / REPLICAS)
    send("w", w_t.at[mat], w_t.at[mat], y_at(2))
    net.expect("w", w_t.at[1 - mat], y_at(2))

    def to_other_core(yy, half):
        part = q_all.at[c, yy, half]
        send("core", part, part, core_peer)

    for half, name in ((near, "near"), (far, "far")):
        for piece in range(len(PIECES)):
            cols = cols_of(piece)
            landing = [net.landing("half%d%d" % (h, piece), q_all.at[c, y, h, :, cols], core_peer) for h in range(2)]

            def land(half=half, landing=landing):
                for h in range(2):
                    pl.when(half == h)(landing[h])

            if name == "far":
                land()
            else:

                @pl.when(owner)
                def _(piece=piece, cols=cols):
                    z_part[zl, :, cols] = q_part[near, :, cols]
                    net.landing("z_sum%d" % piece, z_part.at[pl.ds(0, 3), :, cols], core_peer)()
                    q_all[c, y, near, :, cols] = tree_sum([z_part[i, :, cols] for i in range(4)])

                @pl.when(zl == 2)
                def _(piece=piece):
                    for k in (2, 3, 1):
                        from_owner(1, k, piece).start()

                pl.when(jnp.logical_not(owner))(land)
            part = q_all.at[c, y, half, :, cols]
            for k in (2, 1, 3):
                send("far%d" % k if name == "far" else "near", part, part, y_at(k))
            if name == "near":

                @pl.when(zl == 0)
                def _(piece=piece):
                    for k in (1, 2, 3):
                        from_owner(0, k, piece).start()

        if name == "near":
            net.expect("near", q_all.at[c, pl.ds(0, 3), half], core_peer)
        else:
            for k in (1, 2, 3):
                net.expect("far%d" % k, q_all.at[c, (y + 4 - k) % 4, half], core_peer)
        to_other_core(y, half)
    net.expect("core", q_all.at[1 - c], core_peer)

    def decode_own(yy):
        out = decode(w_out[yy // 2], q_all[c, yy].reshape(RANK, WIDTH))
        cols = pl.ds(pl.multiple_of(yy % 2 * WIDTH, 128), WIDTH)
        decoded[yy // 2, :, cols] = out
        carried[yy // 2, :, cols] = comb[c, yy] - out

    for half, name in ((near, "near"), (far, "far")):
        if name == "near":
            take("near")
        for k in (1, 3, 2):
            if name == "far":
                take("far%d" % k)
            to_other_core((y + 4 - k) % 4, half)
        if name == "near":
            take("w")
            for i in range(MATS):
                hi, lo = split(w_t[i, :, 0:ROWS].T)
                w_out[i] = jnp.concatenate([hi, lo, hi, lo], axis=1)
    for k in (0, 1, 3, 2):
        decode_own((y + 4 - k) % 4)
    net.finish(
        [
            c_recv,
            r1,
            r2,
            p_y.at[pl.ds(0, 7)],
            p_x.at[pl.ds(0, 3)],
            p_z.at[pl.ds(0, 7)],
            p_full.at[pl.ds(0, 16)],
            w_t.at[0],
            q_all.at[0, pl.ds(0, 3)],
            q_all.at[0],
        ],
        core_peer,
    )


def write_kernel(comb, q_all, w_ref, own_decoded, own_carried, decoded, carried, d_buf, c_buf, sem):
    c = lax.axis_index("dp") % 2
    copies = []

    def write(cc, mat, d_ref, c_ref):
        cols = pl.ds(pl.multiple_of(cc * 2 * WIDTH, 128), 2 * WIDTH)
        for ref, to in ((d_ref, decoded.at[mat, :, cols]), (c_ref, carried.at[0, mat, :, cols])):
            copies.append(pltpu.make_async_copy(ref, to, sem.at[0]))
            copies[-1].start()

    for mat in range(MATS):
        write(c, mat, own_decoded.at[mat], own_carried.at[mat])
    for mat in range(MATS):
        for i in range(2):
            cols = pl.ds(i * WIDTH, WIDTH)
            out = decode(w_ref[mat], q_all[1 - c, 2 * mat + i].reshape(RANK, WIDTH))
            d_buf[mat, :, cols] = out
            c_buf[mat, :, cols] = comb[1 - c, 2 * mat + i] - out
        write(1 - c, mat, d_buf.at[mat], c_buf.at[mat])
    for copy in copies:
        copy.wait()


def reduce_call(gradient, feedback, right_initial, name="reduce", collective_id=0):
    right_t = jnp.swapaxes(right_initial, 1, 2)
    vmem = pl.BlockSpec(memory_space=pltpu.VMEM)
    hbm = pl.BlockSpec(memory_space=pltpu.HBM)
    dma = pltpu.SemaphoreType.DMA
    return pl.pallas_call(
        reduce_kernel,
        name=name,
        out_shape=(
            jax.ShapeDtypeStruct((2, 4, ROWS, WIDTH), F32),
            jax.ShapeDtypeStruct((2, 4, 2, 16, WIDTH), F32),
            jax.ShapeDtypeStruct((MATS, ROWS, 128), BF16),
            jax.ShapeDtypeStruct((MATS, ROWS, 2 * WIDTH), F32),
            jax.ShapeDtypeStruct((MATS, ROWS, 2 * WIDTH), F32),
        ),
        in_specs=[hbm] * 3,
        out_specs=(vmem,) * 5,
        scratch_shapes=[
            pltpu.VMEM((4, ROWS, 2 * WIDTH), BF16),
            pltpu.VMEM((4, ROWS, 2 * WIDTH), F32),
            pltpu.VMEM((MATS, RANK, COLS), F32),
            pltpu.VMEM((4, ROWS, WIDTH), F32),
            pltpu.VMEM((4, ROWS, WIDTH), F32),
            pltpu.VMEM((2, HALF, WIDTH), F32),
            pltpu.VMEM((4, HALF, WIDTH), F32),
            pltpu.VMEM((MATS, RANK, 128), F32),
            pltpu.VMEM((8, 16, 128), F32),
            pltpu.VMEM((4, 16, 128), F32),
            pltpu.VMEM((8, 16, 128), F32),
            pltpu.VMEM((RANK, 128), F32),
            pltpu.VMEM((MATS, RANK, 128), F32),
            pltpu.VMEM((2, 16, WIDTH), F32),
            pltpu.VMEM((4, 16, WIDTH), F32),
            dma((5,)),
            dma((1,)),
            dma((TAGS,)),
        ],
        compiler_params=pltpu.CompilerParams(
            collective_id=collective_id, has_side_effects=True, vmem_limit_bytes=VMEM_BYTES
        ),
    )(*(pltpu.with_memory_space_constraint(a, pltpu.HBM) for a in (gradient, feedback, right_t)))


def per_device(gradient, feedback, right_initial):
    vmem = pl.BlockSpec(memory_space=pltpu.VMEM)
    hbm = pl.BlockSpec(memory_space=pltpu.HBM)
    return pl.pallas_call(
        write_kernel,
        name="write",
        out_shape=(
            jax.ShapeDtypeStruct((MATS, ROWS, COLS), F32),
            jax.ShapeDtypeStruct((1, MATS, ROWS, COLS), F32),
        ),
        in_specs=[vmem] * 5,
        out_specs=(hbm, hbm),
        scratch_shapes=[
            pltpu.VMEM((MATS, ROWS, 2 * WIDTH), F32),
            pltpu.VMEM((MATS, ROWS, 2 * WIDTH), F32),
            pltpu.SemaphoreType.DMA((1,)),
        ],
        compiler_params=pltpu.CompilerParams(vmem_limit_bytes=VMEM_BYTES),
    )(*reduce_call(gradient, feedback, right_initial))


def solution(mesh):
    placed = (P("dp", None, None, "mp"), P("dp", None, None, "mp"), P(None, "mp", None))
    return jax.shard_map(
        per_device,
        mesh=mesh,
        in_specs=placed,
        out_specs=(P(None, None, "mp"), P("dp", None, None, "mp")),
        check_vma=False,
    )
```

```python
import jax
import jax.numpy as jnp
from jax import lax
from jax.experimental import pallas as pl
from jax.experimental.pallas import tpu as pltpu
from jax.sharding import PartitionSpec as P

MESH = pl.DeviceIdType.MESH
F32 = jnp.float32
BF16 = jnp.bfloat16
MATS, ROWS, RANK, COLS = 2, 96, 32, 3584
WIDTH = 896
PIECES = ((0, 384), (384, 256), (640, 256))
RING = (pl.ds(0, 640), pl.ds(640, 256))
HALF = ROWS // 2
REPLICAS = 32
BLOCK = 4
TAGS = 26
VMEM_BYTES = 32 << 20


def split(a):
    hi = a.astype(BF16)
    return hi, (a - hi.astype(F32)).astype(BF16)


def dot(a, b, contract):
    return lax.dot_general(a, b, ((contract[0], contract[1]), ((), ())), preferred_element_type=F32)


def exact(a, b, contract):
    return lax.dot_general(
        a, b, ((contract[0], contract[1]), ((), ())), precision=lax.Precision.HIGHEST, preferred_element_type=F32
    )


def left_times_inverse(p_t):
    gram = exact(p_t, p_t, ((1,), (1,)))
    row = lax.broadcasted_iota(jnp.int32, (RANK, RANK), 0)
    col = lax.broadcasted_iota(jnp.int32, (RANK, RANK), 1)
    eye = jnp.where(row == col, 1.0, 0.0).astype(F32)
    inv = eye
    for start in range(0, RANK, BLOCK):
        columns = [jnp.broadcast_to(gram[:, k : k + 1], (RANK, RANK)) for k in range(start, start + BLOCK)]
        for j, k in enumerate(range(start, start + BLOCK)):
            factor = jnp.where(row > k, columns[j] * (1.0 / columns[j][k : k + 1, :]), 0.0)
            gram, inv = (a - factor * a[k : k + 1, :] for a in (gram, inv))
            columns[j + 1 :] = [a - factor * a[k : k + 1, :] for a in columns[j + 1 :]]
    diag = jnp.sum(gram * eye, axis=1, keepdims=True)
    l_inv = inv * lax.rsqrt(diag)
    orth_t = exact(l_inv, p_t, ((1,), (0,)))
    return exact(l_inv, orth_t, ((0,), (0,)))


def decode(left, q):
    hi, lo = split(q)
    return dot(left, jnp.concatenate([hi, hi, lo, lo], axis=0), ((1,), (0,)))


class Net:
    def __init__(self, send_sem, recv_sem):
        self.send_sem, self.recv_sem = send_sem, recv_sem
        self.tags, self.due, self.last = {"": 0}, {}, []

    def copy(self, tag, src, dst, to):
        return pltpu.make_async_remote_copy(
            src_ref=src,
            dst_ref=dst,
            send_sem=self.send_sem.at[0],
            recv_sem=self.recv_sem.at[self.tags.setdefault(tag, len(self.tags))],
            device_id=to,
            device_id_type=MESH,
        )

    def send(self, tag, src, dst, to):
        self.copy(tag, src, dst, to).start()

    def landing(self, tag, ref, to):
        return self.copy(tag, ref, ref, to).wait_recv

    def expect(self, tag, ref, to):
        self.due[tag] = self.landing(tag, ref, to)

    def take(self, tag):
        self.due.pop(tag)()

    def at_end(self, step):
        self.last.append(step)

    def finish(self, totals, to):
        for tag in list(self.due):
            self.take(tag)
        for ref in totals:
            self.copy("", ref, ref, to).wait_send()
        for step in self.last:
            step()


def tree_sum(terms):
    while len(terms) > 1:
        terms = [a + b for a, b in zip(terms[::2], terms[1::2])]
    return terms[0]


def reduce_kernel(
    g_hbm, f_hbm, r_hbm, comb, q_all, w_out, decoded, carried,
    g_buf, f_buf, r_buf, c_recv, s_buf, r1, r2, p_own, p_y, p_x, p_z, p_full, w_t, q_part, z_part,
    load_sem, send_sem, recv_sem,
):
    d = lax.axis_index("dp")
    m = lax.axis_index("mp")
    zl, y, c = d // 8, (d // 2) % 4, d % 2
    x, zh = m // 2, m % 2
    z = zh * 4 + zl
    net = Net(send_sem, recv_sem)
    send, take = net.send, net.take

    def at(zl_=zl, y_=y, c_=c, x_=x, zh_=zh):
        return (zl_ * 8 + y_ * 2 + c_, x_ * 2 + zh_)

    def y_at(k):
        return at(y_=(y + k) % 4)

    def x_at(k):
        return at(x_=(x + k) % 4)

    def z_at(k):
        to = (z + k) % 8
        return at(zl_=to % 4, zh_=to // 4)

    def zl_at(k):
        return at(zl_=(zl + k) % 4)

    core_peer = at(c_=1 - c)
    y_next, y_prev, y_far = (y + 1) % 4, (y + 3) % 4, (y + 2) % 4
    mat = y // 2

    barrier = pltpu.get_barrier_semaphore()

    def greet(peers):
        for to in peers:
            pl.semaphore_signal(barrier, inc=1, device_id=to, device_id_type=MESH)

    z_peers = [z_at(k) for k in (4, 3, 5, 2, 6, 1, 7)]
    greet(z_peers)

    pairs = [(1 - c, 1 - mat), (c, 1 - mat), (1 - c, mat), (c, mat)]
    loads = []
    for i, (cc, mm) in enumerate(pairs):
        cols = pl.ds(pl.multiple_of(cc * 2 * WIDTH, 128), 2 * WIDTH)
        loads.append(
            (
                pltpu.make_async_copy(f_hbm.at[0, mm, :, cols], f_buf.at[i], load_sem.at[i]),
                pltpu.make_async_copy(g_hbm.at[0, mm, :, cols], g_buf.at[i], load_sem.at[i]),
            )
        )
    right_load = pltpu.make_async_copy(r_hbm, r_buf, load_sem.at[4])
    right_load.start()
    for copies in loads:
        for copy in copies:
            copy.start()

    near_peers = [core_peer] + [at(y_=(y + k) % 4, c_=cc) for k in (2, 1, 3) for cc in (c, 1 - c)]
    near_peers += [x_at(k) for k in (2, 1, 3)]
    greet(near_peers)
    p_own[...] = jnp.zeros(p_own.shape, F32)
    p_sums = {}

    def combine(i, yy):
        cc = pairs[i][0]
        cols = pl.ds(pl.multiple_of(yy % 2 * WIDTH, 128), WIDTH)
        comb[cc, yy] = g_buf[i, :, cols].astype(F32) + f_buf[i, :, cols]

    def to_core(name, yy):
        send(name, comb.at[1 - c, yy], c_recv.at[yy], core_peer)

    def sum_cores(yy):
        s_buf[yy] = comb[c, yy] + c_recv[yy]

    def left_product(i, yy):
        hi, lo = split(comb[pairs[i][0], yy])
        cols = pl.ds(pl.multiple_of((2 * pairs[i][0] + yy % 2) * WIDTH, 128), WIDTH)
        right = jnp.concatenate(split(r_buf[yy // 2, :, cols]), axis=0)
        both = dot(jnp.concatenate([hi, lo], axis=0), right, ((1,), (1,)))
        p_sums.setdefault(i // 2, []).append(both[:ROWS] + both[ROWS:])

    def left_sum(i):
        both = tree_sum(p_sums[i]).T
        p_own[mat if i else 1 - mat, :, 0:ROWS] = both[:RANK] + both[RANK:]

    y_beside = mat * 2 + 1 - y % 2
    y_across = (1 - mat) * 2 + 1 - y % 2
    top, low = pl.ds(0, HALF), pl.ds(HALF, HALF)

    def wait_load(i):
        for copy in loads[i]:
            copy.wait()

    ranks = pl.ds(pl.multiple_of(c * 16, 16), 16)
    k_other, k_same = 3 - 2 * (y % 2), 1 + 2 * (y % 2)

    def to_place(k, cc):
        part = p_own.at[(y + k) % 4 // 2, pl.ds(pl.multiple_of(cc * 16, 16), 16)]
        send("p_y", part, p_y.at[2 * y + c], at(y_=(y + k) % 4, c_=cc))

    def other_matrix():
        pl.semaphore_wait(barrier, len(z_peers) + len(near_peers))
        for k in (2, k_other):
            for cc in (c, 1 - c):
                to_place(k, cc)

    right_load.wait()
    for i in range(4):
        wait_load(i)
        for yy in ((y_far, y_across), (y_beside, y))[i // 2]:
            combine(i, yy)
            left_product(i, yy)
        if i % 2 == 1:
            left_sum(i // 2)
            pl.when(z >= 4 if i == 1 else z < 4)(other_matrix)
    to_core("c_far", y_far)
    for cc in (c, 1 - c):
        to_place(k_same, cc)
    to_place(0, 1 - c)
    net.expect("p_y", p_y.at[pl.ds(0, 7)], core_peer)
    p_y[2 * y + c] = p_own[mat, ranks]
    to_core("c_rest", y_across)
    to_core("c_rest", y_beside)
    to_core("c_rest", y)

    def ring_first(part):
        cols = RING[part]
        send("r_far%d" % part, s_buf.at[y_far, top, cols], r1.at[0, :, cols], y_at(1))
        send("r_far%d" % part, s_buf.at[y_far, low, cols], r1.at[1, :, cols], y_at(3))
        net.expect("r_far%d" % part, r1.at[:, :, cols], core_peer)

    def ring_ready(part):
        cols, tag = RING[part], "r_end%d" % part
        send(tag, s_buf.at[y_next, low, cols], r2.at[0, :, cols], y_at(1))
        send(tag, s_buf.at[y_prev, top, cols], r2.at[1, :, cols], y_at(3))

    def ring_second(part):
        cols, tag = RING[part], "r_end%d" % part
        take("r_far%d" % part)
        s_buf[y_next, top, cols] += r1[0, :, cols]
        send(tag, s_buf.at[y_next, top, cols], r2.at[2, :, cols], y_at(1))
        s_buf[y_prev, low, cols] += r1[1, :, cols]
        send(tag, s_buf.at[y_prev, low, cols], r2.at[3, :, cols], y_at(3))
        net.expect(tag, r2.at[:, :, cols], core_peer)

    def ring_end(part):
        cols = RING[part]
        take("r_end%d" % part)
        s_buf[y, top, cols] = (s_buf[y, top, cols] + r2[1, :, cols]) + r2[2, :, cols]
        s_buf[y, low, cols] = (s_buf[y, low, cols] + r2[0, :, cols]) + r2[3, :, cols]

    net.expect("c_far", c_recv.at[0], core_peer)
    net.expect("c_rest", c_recv.at[pl.ds(0, 3)], core_peer)
    take("c_far")
    sum_cores(y_far)
    ring_first(0)
    ring_first(1)

    take("p_y")
    p_x[x] = tree_sum([p_y[i] for i in range(8)])
    for k in (2, 1, 3):
        send("p_x", p_x.at[x], p_x.at[x], x_at(k))
    net.expect("p_x", p_x.at[pl.ds(0, 3)], core_peer)
    take("c_rest")
    sum_cores(y_across)
    sum_cores(y_beside)
    ring_ready(0)

    take("p_x")
    p_z[z] = tree_sum([p_x[i] for i in range(4)])
    for k in (4, 3, 5, 2, 6, 1, 7):
        send("p_z", p_z.at[z], p_z.at[z], z_at(k))
    net.expect("p_z", p_z.at[pl.ds(0, 7)], core_peer)
    ring_second(0)
    ring_ready(1)
    ring_second(1)
    sum_cores(y)
    take("p_z")
    p_full[ranks] = tree_sum([p_z[i] for i in range(8)]) * (1.0 / REPLICAS)
    send("p_full", p_full.at[ranks], p_full.at[ranks], core_peer)
    net.expect("p_full", p_full.at[pl.ds(pl.multiple_of(16 - c * 16, 16), 16)], core_peer)
    ring_end(0)
    halves = [split(s_buf[y, :, pl.ds(*PIECES[piece])]) for piece in range(len(PIECES) - 1)]
    take("p_full")

    near = (zl + 2) // 3
    far = 1 - near
    owner = (zl == 0) | (zl == 2)

    def cols_of(piece):
        return pl.ds(*PIECES[piece])

    def to_owner(h, piece):
        cols = cols_of(piece)
        return net.copy("z_sum%d" % piece, q_part.at[h, :, cols], z_part.at[zl, :, cols], at(zl_=2 * h))

    def from_owner(h, k, piece):
        mine = q_all.at[c, y, h, :, cols_of(piece)]
        return net.copy("half%d%d" % (h, piece), mine, mine, zl_at(k))

    left = jnp.concatenate(split(p_full[:, :ROWS]), axis=0)
    for piece in range(len(PIECES)):
        cols = cols_of(piece)
        if piece == len(PIECES) - 1:
            ring_end(1)
            halves.append(split(s_buf[y, :, cols]))
        hi, lo = halves[piece]
        prod = dot(left, hi, ((1,), (0,))) + dot(left, lo, ((1,), (0,)))
        q_part[:, :, cols] = (prod[:RANK] + prod[RANK:]).reshape(2, 16, PIECES[piece][1])
        for h in range(2):
            pl.when(zl != 2 * h)(to_owner(h, piece).start)

    @net.at_end
    def _():
        def sent(ref):
            net.copy("", ref, ref, core_peer).wait_send()

        sent(q_part.at[0])

        @pl.when(owner)
        def _():
            for _ in range(3):
                sent(q_part.at[0])

        @pl.when(jnp.logical_not(owner))
        def _():
            sent(q_part.at[1])

    w_t[mat, :, 0:ROWS] = left_times_inverse(p_full[:, :ROWS]) * (1.0 / REPLICAS)
    send("w", w_t.at[mat], w_t.at[mat], y_at(2))
    net.expect("w", w_t.at[1 - mat], y_at(2))

    def to_other_core(yy, half):
        part = q_all.at[c, yy, half]
        send("core", part, part, core_peer)

    for half, name in ((near, "near"), (far, "far")):
        for piece in range(len(PIECES)):
            cols = cols_of(piece)
            landing = [net.landing("half%d%d" % (h, piece), q_all.at[c, y, h, :, cols], core_peer) for h in range(2)]

            def land(half=half, landing=landing):
                for h in range(2):
                    pl.when(half == h)(landing[h])

            if name == "far":
                land()
            else:

                @pl.when(owner)
                def _(piece=piece, cols=cols):
                    z_part[zl, :, cols] = q_part[near, :, cols]
                    net.landing("z_sum%d" % piece, z_part.at[pl.ds(0, 3), :, cols], core_peer)()
                    q_all[c, y, near, :, cols] = tree_sum([z_part[i, :, cols] for i in range(4)])

                @pl.when(zl == 2)
                def _(piece=piece):
                    for k in (2, 3, 1):
                        from_owner(1, k, piece).start()

                pl.when(jnp.logical_not(owner))(land)
            part = q_all.at[c, y, half, :, cols]
            for k in (2, 1, 3):
                send("far%d" % k if name == "far" else "near", part, part, y_at(k))
            if name == "near":

                @pl.when(zl == 0)
                def _(piece=piece):
                    for k in (1, 2, 3):
                        from_owner(0, k, piece).start()

        if name == "near":
            net.expect("near", q_all.at[c, pl.ds(0, 3), half], core_peer)
        else:
            for k in (1, 2, 3):
                net.expect("far%d" % k, q_all.at[c, (y + 4 - k) % 4, half], core_peer)
        to_other_core(y, half)
    net.expect("core", q_all.at[1 - c], core_peer)

    def decode_own(yy):
        out = decode(w_out[yy // 2], q_all[c, yy].reshape(RANK, WIDTH))
        cols = pl.ds(pl.multiple_of(yy % 2 * WIDTH, 128), WIDTH)
        decoded[yy // 2, :, cols] = out
        carried[yy // 2, :, cols] = comb[c, yy] - out

    for half, name in ((near, "near"), (far, "far")):
        if name == "near":
            take("near")
        for k in (1, 3, 2):
            if name == "far":
                take("far%d" % k)
            to_other_core((y + 4 - k) % 4, half)
        if name == "near":
            take("w")
            for i in range(MATS):
                hi, lo = split(w_t[i, :, 0:ROWS].T)
                w_out[i] = jnp.concatenate([hi, lo, hi, lo], axis=1)
    for k in (0, 1, 3, 2):
        decode_own((y + 4 - k) % 4)
    net.finish(
        [
            c_recv,
            r1,
            r2,
            p_y.at[pl.ds(0, 7)],
            p_x.at[pl.ds(0, 3)],
            p_z.at[pl.ds(0, 7)],
            p_full.at[pl.ds(0, 16)],
            w_t.at[0],
            q_all.at[0, pl.ds(0, 3)],
            q_all.at[0],
        ],
        core_peer,
    )


def write_kernel(comb, q_all, w_ref, own_decoded, own_carried, decoded, carried, d_buf, c_buf, sem):
    c = lax.axis_index("dp") % 2
    copies = []

    def write(cc, mat, d_ref, c_ref):
        cols = pl.ds(pl.multiple_of(cc * 2 * WIDTH, 128), 2 * WIDTH)
        for ref, to in ((d_ref, decoded.at[mat, :, cols]), (c_ref, carried.at[0, mat, :, cols])):
            copies.append(pltpu.make_async_copy(ref, to, sem.at[0]))
            copies[-1].start()

    for mat in range(MATS):
        write(c, mat, own_decoded.at[mat], own_carried.at[mat])
    for mat in range(MATS):
        for i in range(2):
            cols = pl.ds(i * WIDTH, WIDTH)
            out = decode(w_ref[mat], q_all[1 - c, 2 * mat + i].reshape(RANK, WIDTH))
            d_buf[mat, :, cols] = out
            c_buf[mat, :, cols] = comb[1 - c, 2 * mat + i] - out
        write(1 - c, mat, d_buf.at[mat], c_buf.at[mat])
    for copy in copies:
        copy.wait()


def reduce_call(gradient, feedback, right_initial, name="reduce", collective_id=0):
    right_t = jnp.swapaxes(right_initial, 1, 2)
    vmem = pl.BlockSpec(memory_space=pltpu.VMEM)
    hbm = pl.BlockSpec(memory_space=pltpu.HBM)
    dma = pltpu.SemaphoreType.DMA
    return pl.pallas_call(
        reduce_kernel,
        name=name,
        out_shape=(
            jax.ShapeDtypeStruct((2, 4, ROWS, WIDTH), F32),
            jax.ShapeDtypeStruct((2, 4, 2, 16, WIDTH), F32),
            jax.ShapeDtypeStruct((MATS, ROWS, 128), BF16),
            jax.ShapeDtypeStruct((MATS, ROWS, 2 * WIDTH), F32),
            jax.ShapeDtypeStruct((MATS, ROWS, 2 * WIDTH), F32),
        ),
        in_specs=[hbm] * 3,
        out_specs=(vmem,) * 5,
        scratch_shapes=[
            pltpu.VMEM((4, ROWS, 2 * WIDTH), BF16),
            pltpu.VMEM((4, ROWS, 2 * WIDTH), F32),
            pltpu.VMEM((MATS, RANK, COLS), F32),
            pltpu.VMEM((4, ROWS, WIDTH), F32),
            pltpu.VMEM((4, ROWS, WIDTH), F32),
            pltpu.VMEM((2, HALF, WIDTH), F32),
            pltpu.VMEM((4, HALF, WIDTH), F32),
            pltpu.VMEM((MATS, RANK, 128), F32),
            pltpu.VMEM((8, 16, 128), F32),
            pltpu.VMEM((4, 16, 128), F32),
            pltpu.VMEM((8, 16, 128), F32),
            pltpu.VMEM((RANK, 128), F32),
            pltpu.VMEM((MATS, RANK, 128), F32),
            pltpu.VMEM((2, 16, WIDTH), F32),
            pltpu.VMEM((4, 16, WIDTH), F32),
            dma((5,)),
            dma((1,)),
            dma((TAGS,)),
        ],
        compiler_params=pltpu.CompilerParams(
            collective_id=collective_id, has_side_effects=True, vmem_limit_bytes=VMEM_BYTES
        ),
    )(*(pltpu.with_memory_space_constraint(a, pltpu.HBM) for a in (gradient, feedback, right_t)))


def per_device(gradient, feedback, right_initial):
    vmem = pl.BlockSpec(memory_space=pltpu.VMEM)
    hbm = pl.BlockSpec(memory_space=pltpu.HBM)
    return pl.pallas_call(
        write_kernel,
        name="write",
        out_shape=(
            jax.ShapeDtypeStruct((MATS, ROWS, COLS), F32),
            jax.ShapeDtypeStruct((1, MATS, ROWS, COLS), F32),
        ),
        in_specs=[vmem] * 5,
        out_specs=(hbm, hbm),
        scratch_shapes=[
            pltpu.VMEM((MATS, ROWS, 2 * WIDTH), F32),
            pltpu.VMEM((MATS, ROWS, 2 * WIDTH), F32),
            pltpu.SemaphoreType.DMA((1,)),
        ],
        compiler_params=pltpu.CompilerParams(vmem_limit_bytes=VMEM_BYTES),
    )(*reduce_call(gradient, feedback, right_initial))


def solution(mesh):
    placed = (P("dp", None, None, "mp"), P("dp", None, None, "mp"), P(None, "mp", None))
    return jax.shard_map(
        per_device,
        mesh=mesh,
        in_specs=placed,
        out_specs=(P(None, None, "mp"), P("dp", None, None, "mp")),
        check_vma=False,
    )
```
